128 devices in a mesh: grp: 8 (over y_lo, z), hs: 16 (over y_hi, x, core).
Axes of the slice: x: 4, y: 4 (y_hi: 2, y_lo: 2; y = y_hi * 2 + y_lo), z: 4, core: 2. Of those that a mesh axis runs over, the one named last changes fastest.
Arguments:
- queries: bfloat16 [4096, 8192], P('grp', 'hs'), may hold values from -6 to 6
- d_out: bfloat16 [4096, 8192], P('grp', 'hs'), may hold values from -6 to 6
- suffix_kv: bfloat16 [4096, 2048], P('grp'), may hold values from -6 to 6
- prefix_kv: bfloat16 [16384, 2048], P(None, 'hs'), may hold values from -6 to 6
- kv_weight: bfloat16 [8192, 2048], P('grp'), may hold values from -0.125 to 0.125
- block_ids: int32 [32, 32], P('grp'), may hold values from 0 to 127, as said below
- lengths: int32 [32], P('grp'), may hold values from 32 to 128, as said below
Outputs:
- d_query: bfloat16 [4096, 8192], P('grp', 'hs')
- d_suffix: bfloat16 [4096, 2048], P('grp', 'hs')
- d_prefix: bfloat16 [16384, 8192], P('hs', 'grp')
The draws below stay inside these ranges and needn't reach their ends.
Inputs may be any that keep to these rules, and one draw needn't show every extreme that they name: `block_ids`: each turn names 32 different prefix blocks. `lengths`: one turn has all 128 tokens live.
All inputs are finite; a program needn't handle non-finite values.
Results may differ from the reference program's by a relative error of at most 0.012.
The reference program's roundings to bfloat16 on the way count: a program that leaves them out, or rounds other values in their place, can miss the bound.
Values may be sent and summed in bfloat16 or wider, within the bound.
A program may use at most 128 MiB of HBM per device.

```python
import math
import jax
import jax.numpy as jnp
from jax import lax

D = 8192
HEADS = 64
KV_HEADS = 8
HEAD_DIM = 128
BLOCK = 128
PICKS = 32
PREFIX_BLOCKS = 128
TURN_LEN = 128
TURNS = 32
TURN_TOK = 4096
PREFIX = 16384


def draw_queries(key, part):
    key = jax.random.fold_in(key, 12)
    values = jnp.clip(jax.random.normal(key, (TURN_TOK, HEADS * HEAD_DIM), jnp.float32), -6.0, 6.0)
    return values.astype(jnp.bfloat16)


def draw_prefix_kv(key, part):
    key = jax.random.fold_in(key, 11)
    values = jnp.clip(jax.random.normal(key, (PREFIX, KV_HEADS * 2 * HEAD_DIM), jnp.float32), -6.0, 6.0)
    return values.astype(jnp.bfloat16)


def draw_block_ids(key, part):
    key = jax.random.fold_in(key, 13)
    turn_keys = jax.random.split(key, TURNS)
    picks = jax.vmap(lambda single: jax.random.permutation(single, PREFIX_BLOCKS)[:PICKS])(turn_keys)
    return picks.astype(jnp.int32)


def draw_lengths(key, part):
    key = jax.random.fold_in(key, 14)
    drawn = jax.random.randint(key, (TURNS,), TURN_LEN // 4, TURN_LEN + 1)
    return drawn.at[0].set(TURN_LEN).astype(jnp.int32)


def block_levels(rng, shape, pieces, least, high):
    loudness, own = 1.0, jax.random.fold_in(rng, 6)
    for position, blocks in pieces:
        steps = jnp.exp(jax.random.uniform(jax.random.fold_in(own, position), (blocks,), jnp.float32, least / len(pieces), high / len(pieces)))
        loudness = loudness * jnp.repeat(steps, shape[position] // blocks).reshape([-1 if axis == position else 1 for axis in range(len(shape))])
    return loudness


def gaussian(own_key, shape, scale, bound, pieces=(), held_as=jnp.bfloat16):
    factor_of = block_levels(own_key, shape, pieces, -0.22, 0.18) if pieces else 1.0
    entries = jax.random.normal(own_key, shape, jnp.float32) * scale * factor_of
    return jnp.minimum(jnp.maximum(entries, -bound), bound).astype(held_as)


def setup_inputs(seed: int = 0) -> dict:
    key_list = jax.random.split(jax.random.key(seed), 8)
    queries = draw_queries(jax.random.fold_in(key_list[7], 71), 0)
    d_out = gaussian(key_list[1], (TURN_TOK, HEADS * HEAD_DIM), 1.0, 6.0, ((0, 8), (1, 16)))
    suffix_kv = gaussian(key_list[2], (TURN_TOK, KV_HEADS * 2 * HEAD_DIM), 1.0, 6.0, ((0, 8),))
    prefix_kv = draw_prefix_kv(jax.random.fold_in(key_list[7], 71), 0)
    kv_weight = gaussian(key_list[4], (D, KV_HEADS * 2 * HEAD_DIM), (KV_HEADS * 2 * HEAD_DIM) ** -0.5, 0.125, ((0, 8),))
    block_ids = draw_block_ids(jax.random.fold_in(key_list[7], 71), 0)
    lengths = draw_lengths(jax.random.fold_in(key_list[7], 71), 0)
    return {"queries": queries, "d_out": d_out, "suffix_kv": suffix_kv, "prefix_kv": prefix_kv, "kv_weight": kv_weight, "block_ids": block_ids, "lengths": lengths}


def turn_keys(block_list):
    offsets = jnp.arange(BLOCK, dtype=jnp.int32)
    return (block_list[:, None].astype(jnp.int32) * BLOCK + offsets[None, :]).reshape(-1)

def reference(queries, d_out, suffix_kv, prefix_kv, kv_weight, block_ids, lengths):
    turns = queries.shape[0] // TURN_LEN
    group = HEADS // KV_HEADS
    picked = PICKS * BLOCK
    width = picked + TURN_LEN
    inv_root = 1.0 / math.sqrt(HEAD_DIM)
    highest = lax.Precision.HIGHEST
    positions = jnp.arange(TURN_LEN, dtype=jnp.int32)

    def step(running, item):
        query_turn, grad_turn, suffix_turn, block_list, length = item
        prefix_rows = turn_keys(block_list)
        key_rows = jnp.concatenate([prefix_kv[prefix_rows], suffix_turn], 0).astype(jnp.float32)
        key_rows = key_rows.reshape(width, KV_HEADS, 2, HEAD_DIM)
        key_part = key_rows[:, :, 0]
        value_part = key_rows[:, :, 1]
        live = positions < length
        grad_live = jnp.where(live[:, None], grad_turn, jnp.zeros_like(grad_turn))
        grad_four = grad_live.astype(jnp.float32).reshape(TURN_LEN, KV_HEADS, group, HEAD_DIM)
        query_four = query_turn.astype(jnp.float32).reshape(TURN_LEN, KV_HEADS, group, HEAD_DIM)
        scores = jnp.einsum('qkgd,nkd->kgqn', query_four, key_part, precision=highest) * inv_root
        causal = (positions[None, :] <= positions[:, None]) & (positions[None, :] < length)
        allowed = jnp.concatenate([jnp.ones((TURN_LEN, picked), dtype=bool), causal], 1)
        scores = jnp.where(allowed, scores, -jnp.inf)
        top_score = lax.optimization_barrier(jnp.max(scores, axis=-1, keepdims=True))
        expon = jnp.exp(scores - top_score)
        probs = expon / lax.optimization_barrier(jnp.sum(expon, axis=-1, keepdims=True))
        probs_low = lax.optimization_barrier(probs.astype(jnp.bfloat16)).astype(jnp.float32)
        output = jnp.einsum('kgqn,nkd->kgqd', probs_low, value_part, precision=highest)
        row_dot = jnp.einsum('qkgd,kgqd->kgq', grad_four, output, precision=highest)
        grad_probs = jnp.einsum('qkgd,nkd->kgqn', grad_four, value_part, precision=highest)
        grad_scores = probs * (grad_probs - row_dot[..., None])
        scores_low = lax.optimization_barrier(grad_scores.astype(jnp.bfloat16)).astype(jnp.float32)
        grad_query = jnp.einsum('kgqn,nkd->qkgd', scores_low, key_part, precision=highest) * inv_root
        grad_key = jnp.einsum('kgqn,qkgd->nkd', scores_low, query_four, precision=highest) * inv_root
        grad_value = jnp.einsum('kgqn,qkgd->nkd', probs_low, grad_four, precision=highest)
        grad_rows = jnp.stack([grad_key, grad_value], 2).reshape(width, KV_HEADS * 2 * HEAD_DIM)
        running = running.at[prefix_rows].add(grad_rows[:picked])
        query_out = grad_query.reshape(TURN_LEN, HEADS * HEAD_DIM).astype(jnp.bfloat16)
        return (running, (query_out, grad_rows[picked:].astype(jnp.bfloat16)))
    start = jnp.zeros((prefix_kv.shape[0], KV_HEADS * 2 * HEAD_DIM), jnp.float32)
    items = (queries.reshape(turns, TURN_LEN, -1), d_out.reshape(turns, TURN_LEN, -1), suffix_kv.reshape(turns, TURN_LEN, -1), block_ids, lengths)
    running, (query_all, suffix_all) = lax.scan(step, start, items)
    prefix_grad = running.astype(jnp.bfloat16)
    d_prefix = jnp.dot(prefix_grad, kv_weight.T, preferred_element_type=jnp.float32).astype(jnp.bfloat16)
    d_query = query_all.reshape(turns * TURN_LEN, HEADS * HEAD_DIM)
    d_suffix = suffix_all.reshape(turns * TURN_LEN, KV_HEADS * 2 * HEAD_DIM)
    return (d_query, d_suffix, d_prefix)
```

```python
import functools
import math

import jax
import jax.numpy as jnp
from jax import lax
from jax.experimental import pallas as pl
from jax.experimental.pallas import tpu as pltpu
from jax.sharding import PartitionSpec as P

HEADS = 64
KV_HEADS = 8
HEAD_DIM = 128
BLOCK = 128
PICKS = 32
TURN_LEN = 128
PREFIX = 16384
PREFIX_BLOCKS = 128

OWN_HEADS = 4
TURNS = 2
ROWS = 2 * OWN_HEADS * TURN_LEN
PICKED = PICKS * BLOCK
KEYS = PICKED + TURN_LEN
PAIR = 2
STEP = PAIR * BLOCK
STEPS = PICKS // PAIR
SLOTS = PICKS + 1
INV_ROOT = 1.0 / math.sqrt(HEAD_DIM)
EXP_SCALE = INV_ROOT * math.log2(math.e)
F32 = jnp.float32
BF16 = jnp.bfloat16
MIB = 1 << 20
HBM = pl.BlockSpec(memory_space=pl.ANY)
SMEM = pl.BlockSpec(memory_space=pltpu.SMEM)
VMEM = pl.BlockSpec(memory_space=pltpu.VMEM)


def dot(a, b, ca, cb):
    return lax.dot_general(a, b, (((ca,), (cb,)), ((), ())), preferred_element_type=F32)


def fold(x, op):
    return op(x.reshape(x.shape[0] // 8, 8, x.shape[1]), axis=0)


def attention_turn(t, turn, ids, inv, lens, kv, qs, gs, suf, score, gval, grad, dq):
    length = lens[turn]

    def block(which, pick):
        return kv[which, ids[turn, pick], :, :]

    def blocks(which, i):
        return jnp.concatenate([block(which, i * PAIR + p) for p in range(PAIR)], 0)

    def rows(i):
        return pl.ds(pl.multiple_of(i * STEP, STEP), STEP)

    own = pl.ds(PICKED, TURN_LEN)
    own_key = suf[pl.ds(pl.multiple_of(t * TURN_LEN, TURN_LEN), TURN_LEN), :HEAD_DIM]
    own_value = suf[pl.ds(pl.multiple_of(t * TURN_LEN, TURN_LEN), TURN_LEN), HEAD_DIM:]

    s = dot(own_key, qs[...], 1, 1)
    key_pos = lax.broadcasted_iota(jnp.int32, s.shape, 0)
    query_pos = lax.rem(lax.broadcasted_iota(jnp.int32, s.shape, 1), TURN_LEN)
    s = jnp.where((key_pos <= query_pos) & (key_pos < length), s, -1e30)
    score[own, :] = s

    def scores(i, top):
        s = dot(blocks(0, i), qs[...], 1, 1)
        score[rows(i), :] = s
        return jnp.maximum(top, fold(s, jnp.max))

    top = lax.fori_loop(0, STEPS, scores, fold(s, jnp.max))
    top = jnp.max(top, axis=0, keepdims=True) * EXP_SCALE

    e = jnp.exp2(score[own, :] * EXP_SCALE - top)
    score[own, :] = e
    gval[own, :] = dot(own_value, gs[...], 1, 1)

    def exponentials(i, total):
        gval[rows(i), :] = dot(blocks(1, i), gs[...], 1, 1)
        e = jnp.exp2(score[rows(i), :] * EXP_SCALE - top)
        score[rows(i), :] = e
        return total + fold(e, jnp.sum)

    total = lax.fori_loop(0, STEPS, exponentials, fold(e, jnp.sum))
    scale = 1.0 / jnp.sum(total, axis=0, keepdims=True)

    def value_grads(where):
        p = score[where, :] * scale
        score[where, :] = p
        low = p.astype(BF16)
        return dot(low, gs[...], 1, 0), fold(low.astype(F32) * gval[where, :], jnp.sum)

    dv, row_dot = value_grads(own)
    grad[t, PICKS, :, HEAD_DIM:] = dv

    def probabilities(i, row_dot):
        dv, more = value_grads(rows(i))
        for p in range(PAIR):
            grad[t, i * PAIR + p, :, HEAD_DIM:] = dv[p * BLOCK:(p + 1) * BLOCK]
        return row_dot + more

    row_dot = lax.fori_loop(0, STEPS, probabilities, row_dot)
    row_dot = jnp.sum(row_dot, axis=0, keepdims=True)

    def key_grads(where, key):
        low = (score[where, :] * (gval[where, :] - row_dot)).astype(BF16)
        return dot(low, qs[...], 1, 0) * INV_ROOT, dot(low, key, 0, 0)

    dk, dq_part = key_grads(own, own_key)
    grad[t, PICKS, :, :HEAD_DIM] = dk
    dq[...] = dq_part

    def gradients(i, carry):
        dk, dq_part = key_grads(rows(i), blocks(0, i))
        for p in range(PAIR):
            grad[t, i * PAIR + p, :, :HEAD_DIM] = dk[p * BLOCK:(p + 1) * BLOCK]
        dq[...] += dq_part
        return carry

    lax.fori_loop(0, STEPS, gradients, 0)


def attention_kernel(
    exchange,
    ids, inv, lens, q_hbm, g_hbm, suf_hbm, kv_hbm,
    dq_hbm, dsuf_hbm, dense_hbm,
    kv, q_own, q_peer, g_own, g_peer, qs, gs, suf, score, gval, grad, dq, dq_own, dq_peer, dsuf, tile,
    in_sems, send_sems, recv_sems, out_sems, tile_sems,
):
    core = lax.rem(lax.axis_index("hs"), 2) if exchange else 0
    head = lax.axis_index("hs") // 2 if exchange else 0
    peer = lax.axis_index("hs") + 1 - 2 * core if exchange else 0
    half = TURNS * TURN_LEN

    def own_rows(c):
        return pl.ds(pl.multiple_of(c * half, half), half)

    def remote(index, source, target):
        if exchange:
            return pltpu.make_async_remote_copy(
                source, target, send_sems.at[index], recv_sems.at[index],
                device_id={"hs": peer}, device_id_type=pl.DeviceIdType.MESH,
            )
        return pltpu.make_async_copy(source, target, send_sems.at[index])

    if exchange:
        barrier = pltpu.get_barrier_semaphore()
        pl.semaphore_signal(
            barrier, inc=1, device_id={"hs": peer}, device_id_type=pl.DeviceIdType.MESH
        )
    columns = pl.ds(pl.multiple_of(head * 2 * HEAD_DIM, 2 * HEAD_DIM), 2 * HEAD_DIM)
    local = [
        pltpu.make_async_copy(kv_hbm, kv.at[core], in_sems.at[0]),
        pltpu.make_async_copy(q_hbm.at[own_rows(core), :], q_own, in_sems.at[1]),
        pltpu.make_async_copy(g_hbm.at[own_rows(core), :], g_own, in_sems.at[2]),
        pltpu.make_async_copy(suf_hbm.at[own_rows(core), columns], suf, in_sems.at[3]),
    ]
    for copy in local:
        copy.start()
    if exchange:
        pl.semaphore_wait(barrier, 1)
    far = [
        remote(0, q_hbm.at[own_rows(1 - core), :], q_peer),
        remote(1, g_hbm.at[own_rows(1 - core), :], g_peer),
        remote(2, kv_hbm, kv.at[core if exchange else 1]),
    ]
    for copy in far:
        copy.start()
    for t in range(TURNS):
        grad[t, SLOTS, :, :] = jnp.zeros((BLOCK, 2 * HEAD_DIM), F32)
    for copy in local:
        copy.wait()
    for copy in far:
        copy.wait()

    def turn_step(t, carry):
        turn = core * TURNS + t
        where = pl.ds(pl.multiple_of(t * TURN_LEN, TURN_LEN), TURN_LEN)
        live = lax.broadcasted_iota(jnp.int32, (TURN_LEN, HEAD_DIM), 0) < lens[turn]
        for j in range(2 * OWN_HEADS):
            q_from, g_from = (q_own, g_own) if j < OWN_HEADS else (q_peer, g_peer)
            lanes = slice(j % OWN_HEADS * HEAD_DIM, (j % OWN_HEADS + 1) * HEAD_DIM)
            here = slice(j * TURN_LEN, (j + 1) * TURN_LEN)
            qs[here, :] = q_from[where, lanes]
            g = g_from[where, lanes]
            gs[here, :] = jnp.where(live, g, jnp.zeros_like(g))
        attention_turn(t, turn, ids, inv, lens, kv, qs, gs, suf, score, gval, grad, dq)
        for j in range(2 * OWN_HEADS):
            target = dq_own if j < OWN_HEADS else dq_peer
            lanes = slice(j % OWN_HEADS * HEAD_DIM, (j % OWN_HEADS + 1) * HEAD_DIM)
            here = slice(j * TURN_LEN, (j + 1) * TURN_LEN)
            target[where, lanes] = (dq[here, :] * INV_ROOT).astype(BF16)
        dsuf[0, where, :] = grad[t, PICKS, :, :HEAD_DIM].astype(BF16)
        dsuf[1, where, :] = grad[t, PICKS, :, HEAD_DIM:].astype(BF16)
        return carry

    lax.fori_loop(0, TURNS, turn_step, 0)

    out = [
        pltpu.make_async_copy(dq_own, dq_hbm.at[own_rows(core), :], out_sems.at[0]),
        pltpu.make_async_copy(dsuf.at[core], dsuf_hbm.at[own_rows(core), :], out_sems.at[1]),
        remote(3, dq_peer, dq_hbm.at[own_rows(core), :] if exchange else dq_hbm.at[own_rows(1), :]),
        remote(4, dsuf.at[1 - core], dsuf_hbm.at[own_rows(core), :] if exchange else dsuf_hbm.at[own_rows(1), :]),
    ]
    for copy in out:
        copy.start()

    def slot_copy(i):
        slot = lax.rem(i, 2)
        return pltpu.make_async_copy(
            tile.at[slot],
            dense_hbm.at[pl.ds(pl.multiple_of(i * 8 * BLOCK, 8 * BLOCK), 8 * BLOCK), :],
            tile_sems.at[slot],
        )

    def dense_step(i, carry):
        @pl.when(i >= 2)
        def _():
            slot_copy(i - 2).wait()

        slot = lax.rem(i, 2)
        for b in range(8):
            acc = None
            for t in range(TURNS):
                part = grad[t, inv[core * TURNS + t, i * 8 + b], :, :]
                acc = part if acc is None else acc + part
            tile[slot, b * BLOCK:(b + 1) * BLOCK, :] = acc.astype(BF16)
        slot_copy(i).start()
        return carry

    count = PREFIX_BLOCKS // 8
    lax.fori_loop(0, count, dense_step, 0)
    slot_copy(count - 2).wait()
    slot_copy(count - 1).wait()
    for copy in out:
        copy.wait()


def attention(ids, inv, lens, q, g, suf, kv, exchange=True):
    half = TURNS * TURN_LEN
    width = OWN_HEADS * HEAD_DIM
    scratch = [
        pltpu.VMEM((2, PREFIX_BLOCKS, BLOCK, HEAD_DIM), BF16),
        pltpu.VMEM((half, width), BF16),
        pltpu.VMEM((half, width), BF16),
        pltpu.VMEM((half, width), BF16),
        pltpu.VMEM((half, width), BF16),
        pltpu.VMEM((ROWS, HEAD_DIM), BF16),
        pltpu.VMEM((ROWS, HEAD_DIM), BF16),
        pltpu.VMEM((half, 2 * HEAD_DIM), BF16),
        pltpu.VMEM((KEYS, ROWS), F32),
        pltpu.VMEM((KEYS, ROWS), F32),
        pltpu.VMEM((TURNS, SLOTS + 1, BLOCK, 2 * HEAD_DIM), F32),
        pltpu.VMEM((ROWS, HEAD_DIM), F32),
        pltpu.VMEM((half, width), BF16),
        pltpu.VMEM((half, width), BF16),
        pltpu.VMEM((2, half, HEAD_DIM), BF16),
        pltpu.VMEM((2, 8 * BLOCK, 2 * HEAD_DIM), BF16),
        pltpu.SemaphoreType.DMA((4,)),
        pltpu.SemaphoreType.DMA((5,)),
        pltpu.SemaphoreType.DMA((5,)),
        pltpu.SemaphoreType.DMA((2,)),
        pltpu.SemaphoreType.DMA((2,)),
    ]
    return pl.pallas_call(
        functools.partial(attention_kernel, exchange),
        out_shape=[
            jax.ShapeDtypeStruct((2 * half, width), BF16),
            jax.ShapeDtypeStruct((2 * half, HEAD_DIM), BF16),
            jax.ShapeDtypeStruct((PREFIX, 2 * HEAD_DIM), BF16),
        ],
        in_specs=[SMEM, SMEM, SMEM, HBM, HBM, HBM, HBM],
        out_specs=[HBM, HBM, HBM],
        scratch_shapes=scratch,
        compiler_params=pltpu.CompilerParams(
            collective_id=0 if exchange else None,
            has_side_effects=True,
            vmem_limit_bytes=62 * MIB,
        ),
        name="attention",
    )(ids, inv, lens, q, g, suf, kv.reshape(PREFIX_BLOCKS, BLOCK, HEAD_DIM))


RANGE = PREFIX // (2 * KV_HEADS)
PARTS = 8
CHUNK = RANGE // PARTS
HALF = CHUNK // 2
KV_WIDTH = 2 * HEAD_DIM
SET = KV_HEADS // 2
PIECES = 2
PIECE = SET // PIECES


def reduce_kernel(
    dense_hbm, w_hbm, out,
    acc, r_core, r_y0, r_z10, r_z20, r_z11, r_z21, r_y1, x, w,
    in_sems, w_sem, s_core, s_y0, s_z10, s_z20, s_z11, s_z21, s_y1, s_t, s_g0, s_g1, s_own,
):
    hs = lax.axis_index("hs")
    grp = lax.axis_index("grp")
    core, head = lax.rem(hs, 2), hs // 2
    y, z = grp // 4, lax.rem(grp, 4)
    zs = (lax.rem(z + 1, 4), lax.rem(z + 3, 4))
    zo = lax.rem(z + 2, 4)
    to_core = {"hs": head * 2 + 1 - core}
    to_y = {"grp": (1 - y) * 4 + z}
    to_z = [{"grp": y * 4 + zs[0]}, {"grp": y * 4 + zs[1]}]

    def remote(source, target, sems, index, device):
        return pltpu.make_async_remote_copy(
            source, target, sems.at[(0, *index)], sems.at[(1, *index)],
            device_id=device, device_id_type=pl.DeviceIdType.MESH,
        )

    def range_rows(c, k):
        return pl.ds(pl.multiple_of((c * 2 + k) * RANGE, RANGE), RANGE)

    def own_in(c):
        return pltpu.make_async_copy(dense_hbm.at[range_rows(c, core), :], acc.at[c], in_sems.at[c])

    def core_copy(c):
        return remote(dense_hbm.at[range_rows(c, 1 - core), :], r_core.at[c], s_core, (c,), to_core)

    def chunk_rows(part, count=1):
        return pl.ds(pl.multiple_of(part * CHUNK, CHUNK), count * CHUNK)

    def half_rows(part, d):
        return pl.ds(pl.multiple_of(part * CHUNK + d * HALF, HALF), HALF)

    def y0(i):
        return remote(acc.at[i, chunk_rows((1 - y) * 4, 4), :], r_y0.at[i], s_y0, (i,), to_y)

    def z10(i, d):
        return remote(acc.at[i, half_rows(y * 4 + zo, d), :], r_z10.at[i, d], s_z10, (i, d), to_z[d])

    def z20(i, d):
        return remote(acc.at[i, chunk_rows(y * 4 + zs[d]), :], r_z20.at[i, d], s_z20, (i, d), to_z[d])

    def z11(i, d, v):
        return remote(acc.at[SET + i, half_rows(v * 4 + zo, d), :], r_z11.at[i, d, v], s_z11, (i, d, v), to_z[d])

    def z21(i, d, v):
        return remote(acc.at[SET + i, chunk_rows(v * 4 + zs[d]), :], r_z21.at[i, d, v], s_z21, (i, d, v), to_z[d])

    def y1(i):
        return remote(acc.at[SET + i, chunk_rows((1 - y) * 4 + z), :], r_y1.at[i], s_y1, (i,), to_y)

    def turn_out(c):
        return pltpu.make_async_remote_copy(
            acc.at[c, chunk_rows(grp), :], x.at[head, chunk_rows(grp), :], s_t.at[0, c], s_t.at[1, head],
            device_id={"hs": c * 2 + core}, device_id_type=pl.DeviceIdType.MESH,
        )

    def turn_in(c):
        return pltpu.make_async_remote_copy(
            acc.at[c, chunk_rows(grp), :], x.at[c, chunk_rows(grp), :], s_t.at[0, c], s_t.at[1, c],
            device_id={"hs": c * 2 + core}, device_id_type=pl.DeviceIdType.MESH,
        )

    def turn_own(c):
        return pltpu.make_async_copy(acc.at[c, chunk_rows(grp), :], x.at[c, chunk_rows(grp), :], s_own)

    def each(count, body):
        def step(i, carry):
            body(i)
            return carry

        lax.fori_loop(0, count, step, 0)

    def add(c, rows, *terms):
        total = acc[c, rows, :].astype(F32)
        for term in terms:
            total = total + term.astype(F32)
        acc[c, rows, :] = total.astype(BF16)

    barrier = pltpu.get_barrier_semaphore()

    def greet(device):
        pl.semaphore_signal(barrier, inc=1, device_id=device, device_id_type=pl.DeviceIdType.MESH)

    for device in (to_core, to_y, *to_z):
        greet(device)
    for j in range(1, KV_HEADS):
        greet({"hs": lax.rem(head + j, KV_HEADS) * 2 + core})
    w_copy = pltpu.make_async_copy(w_hbm, w, w_sem)

    def start_own(i):
        own_in(i).start()
        own_in(SET + i).start()

    each(SET, start_own)
    pl.semaphore_wait(barrier, 3 + KV_HEADS)

    def start_core(i):
        core_copy(i).start()
        core_copy(SET + i).start()

    each(SET, start_core)
    w_copy.start()

    def sum_cores(i):
        for c in (i, SET + i):
            own_in(c).wait()
            core_copy(c).wait_recv()
            acc[c, :, :] = acc[c, :, :] + r_core[c, :, :]
        y0(i).start()
        for d in range(2):
            for v in range(2):
                z11(i, d, v).start()

    each(SET, sum_cores)

    def second(i):
        for d in range(2):
            for v in range(2):
                z11(i, d, v).wait_recv()
                add(SET + i, half_rows(v * 4 + zs[d], d), r_z11[i, d, v])
        for d in range(2):
            for v in range(2):
                z21(i, d, v).start()
        y0(i).wait_recv()
        add(i, chunk_rows(y * 4, 4), r_y0[i])
        for d in range(2):
            z10(i, d).start()

    each(SET, second)

    def third(i):
        for d in range(2):
            for v in range(2):
                z21(i, d, v).wait_recv()
        for v in range(2):
            add(SET + i, chunk_rows(v * 4 + z), r_z21[i, 0, v], r_z21[i, 1, v])
        y1(i).start()
        for d in range(2):
            z10(i, d).wait_recv()
            add(i, half_rows(y * 4 + zs[d], d), r_z10[i, d])
        for d in range(2):
            z20(i, d).start()

    each(SET, third)

    def hand_on(c):
        @pl.when(c != head)
        def _():
            turn_out(c).start()

        @pl.when(c == head)
        def _():
            turn_own(c).start()

    def fourth(i):
        for d in range(2):
            z20(i, d).wait_recv()
        add(i, chunk_rows(grp), r_z20[i, 0], r_z20[i, 1])
        hand_on(i)
        y1(i).wait_recv()
        add(SET + i, chunk_rows(grp), r_y1[i])
        hand_on(SET + i)

    each(SET, fourth)

    def part(v, place):
        return v * 4 + place

    def g_copy(sems, index, base, p, rows, device):
        where = x.at[pl.ds(base + p * PIECE, PIECE), rows, :]
        return remote(where, where, sems, (p, index), device)

    def gy0(p):
        return g_copy(s_g0, 0, 0, p, chunk_rows(grp), to_y)

    def gz10(p, d, far):
        return g_copy(s_g0, 1 + d + 2 * far, 0, p, chunk_rows(part(1 - y if far else y, z)), to_z[d])

    def gz20(p, d, far):
        return g_copy(s_g0, 5 + d + 2 * far, 0, p, half_rows(part(1 - y if far else y, zs[1 - d]), d), to_z[d])

    def gz11(p, d):
        return g_copy(s_g1, d, SET, p, chunk_rows(grp), to_z[d])

    def gz21(p, d):
        return g_copy(s_g1, 2 + d, SET, p, half_rows(part(y, zs[1 - d]), d), to_z[d])

    def gy1(p, which):
        place = (z, zs[0], zs[1], zo)[which]
        return g_copy(s_g1, 4 + which, SET, p, chunk_rows(part(y, place)), to_y)

    def arrived(c):
        @pl.when(c != head)
        def _():
            turn_in(c).wait_recv()

        @pl.when(c == head)
        def _():
            turn_own(c).wait()

    def gather_first(p):
        for j in range(PIECE):
            arrived(p * PIECE + j)
        gy0(p).start()
        for d in range(2):
            gz10(p, d, False).start()
        for j in range(PIECE):
            arrived(SET + p * PIECE + j)
        for d in range(2):
            gz11(p, d).start()
        gy1(p, 0).start()

    each(PIECES, gather_first)
    w_copy.wait()

    def product(place, count=1):
        rows = chunk_rows(place, count)
        left = jnp.concatenate([x[c, rows, :] for c in range(KV_HEADS)], 1)
        out[rows, :] = dot(left, w[...], 1, 1).astype(BF16)

    def gather_second(p):
        gy0(p).wait_recv()
        for d in range(2):
            gz10(p, d, True).start()
        for d in range(2):
            gz11(p, d).wait_recv()
            gy1(p, 2 - d).start()
            gz21(p, d).start()
        for d in range(2):
            gz10(p, d, False).wait_recv()
            gz20(p, d, False).start()

    each(PIECES, gather_second)
    product(grp)

    def gather_third(p):
        for d in range(2):
            gz21(p, d).wait_recv()
        gy1(p, 3).start()
        for d in range(2):
            gz10(p, d, True).wait_recv()
            gz20(p, d, True).start()

    each(PIECES, gather_third)
    product(part(y, zs[0]))
    product(part(y, zs[1]))

    def gather_fourth(p):
        for d in range(2):
            gz20(p, d, False).wait_recv()
            gz20(p, d, True).wait_recv()
        for which in range(4):
            gy1(p, which).wait_recv()

    each(PIECES, gather_fourth)
    product(part(y, zo))
    product(part(1 - y, 0), 4)

    def sent_sets(i):
        core_copy(i).wait_send()
        core_copy(SET + i).wait_send()
        y0(i).wait_send()
        y1(i).wait_send()
        for d in range(2):
            z10(i, d).wait_send()
            z20(i, d).wait_send()
            for v in range(2):
                z11(i, d, v).wait_send()
                z21(i, d, v).wait_send()

    each(SET, sent_sets)

    def sent_turn(c):
        @pl.when(c != head)
        def _():
            turn_out(c).wait_send()

    each(KV_HEADS, sent_turn)

    def sent_gather(p):
        gy0(p).wait_send()
        for d in range(2):
            gz11(p, d).wait_send()
            gz21(p, d).wait_send()
            for far in (False, True):
                gz10(p, d, far).wait_send()
                gz20(p, d, far).wait_send()
        for which in range(4):
            gy1(p, which).wait_send()

    each(PIECES, sent_gather)


def reduce_and_project(dense, weight):
    width = KV_HEADS * KV_WIDTH
    dma = pltpu.SemaphoreType.DMA
    scratch = [
        pltpu.VMEM((KV_HEADS, RANGE, KV_WIDTH), BF16),
        pltpu.VMEM((KV_HEADS, RANGE, KV_WIDTH), BF16),
        pltpu.VMEM((SET, 4 * CHUNK, KV_WIDTH), BF16),
        pltpu.VMEM((SET, 2, HALF, KV_WIDTH), BF16),
        pltpu.VMEM((SET, 2, CHUNK, KV_WIDTH), BF16),
        pltpu.VMEM((SET, 2, 2, HALF, KV_WIDTH), BF16),
        pltpu.VMEM((SET, 2, 2, CHUNK, KV_WIDTH), BF16),
        pltpu.VMEM((SET, CHUNK, KV_WIDTH), BF16),
        pltpu.VMEM((KV_HEADS, RANGE, KV_WIDTH), BF16),
        pltpu.VMEM(weight.shape, BF16),
        dma((KV_HEADS,)),
        dma,
        dma((2, KV_HEADS)),
        dma((2, SET)),
        dma((2, SET, 2)),
        dma((2, SET, 2)),
        dma((2, SET, 2, 2)),
        dma((2, SET, 2, 2)),
        dma((2, SET)),
        dma((2, KV_HEADS)),
        dma((2, PIECES, 9)),
        dma((2, PIECES, 8)),
        dma,
    ]
    return pl.pallas_call(
        reduce_kernel,
        out_shape=jax.ShapeDtypeStruct((RANGE, weight.shape[0]), BF16),
        in_specs=[HBM, HBM],
        out_specs=VMEM,
        scratch_shapes=scratch,
        compiler_params=pltpu.CompilerParams(
            collective_id=1, has_side_effects=True, vmem_limit_bytes=48 * MIB
        ),
        name="reduce_and_project",
    )(dense, weight)


def on_device(queries, d_out, suffix_kv, prefix_kv, kv_weight, block_ids, lengths):
    blocks = jnp.arange(PREFIX_BLOCKS, dtype=jnp.int32)
    picks = jnp.arange(PICKS, dtype=jnp.int32) - SLOTS
    named = block_ids[:, :, None] == blocks
    inverse = jnp.sum(jnp.where(named, picks[None, :, None], 0), axis=1) + SLOTS
    d_query, d_suffix, dense = attention(
        block_ids, inverse, lengths, queries, d_out, suffix_kv, prefix_kv
    )
    return d_query, d_suffix, reduce_and_project(dense, kv_weight)


def solution(mesh):
    placed = (
        P("grp", "hs"),
        P("grp", "hs"),
        P("grp", None),
        P(None, "hs"),
        P("grp", None),
        P("grp", None),
        P("grp"),
    )
    return jax.shard_map(
        on_device,
        mesh=mesh,
        in_specs=placed,
        out_specs=(P("grp", "hs"), P("grp", "hs"), P("hs", "grp")),
        check_vma=False,
    )
```

```python
import functools
import math

import jax
import jax.numpy as jnp
from jax import lax
from jax.experimental import pallas as pl
from jax.experimental.pallas import tpu as pltpu
from jax.sharding import PartitionSpec as P

KV_HEADS = 8
HEAD_DIM = 128
BLOCK = 128
PICKS = 32
TURN_LEN = 128
PREFIX = 16384
PREFIX_BLOCKS = 128

OWN_HEADS = 4
TURNS = 2
MINE = TURNS * TURN_LEN
ROWS = 2 * OWN_HEADS * TURN_LEN
PICKED = PICKS * BLOCK
KEYS = PICKED + TURN_LEN
GROUP = 8
STEP = GROUP * BLOCK
STEPS = PICKS // GROUP
SLOTS = PICKS + 1
INV_ROOT = 1.0 / math.sqrt(HEAD_DIM)
EXP_SCALE = INV_ROOT * math.log2(math.e)
RANGE = PREFIX // (2 * KV_HEADS)
RANGE_BLOCKS = RANGE // BLOCK
PARTS = 8
CHUNK = RANGE // PARTS
HALF = CHUNK // 2
SET = KV_HEADS // 2
PIECES = 2
PIECE = SET // PIECES
F32 = jnp.float32
BF16 = jnp.bfloat16
MIB = 1 << 20
MESH = pl.DeviceIdType.MESH
HBM = pl.BlockSpec(memory_space=pl.ANY)
SMEM = pl.BlockSpec(memory_space=pltpu.SMEM)


def dot(a, b, ca, cb):
    return lax.dot_general(a, b, (((ca,), (cb,)), ((), ())), preferred_element_type=F32)


def fold(x, op):
    return op(x.reshape(x.shape[0] // 8, 8, x.shape[1]), axis=0)


def each(count, body):
    def step(i, carry):
        body(i)
        return carry

    lax.fori_loop(0, count, step, 0)


def aligned(start, size):
    return pl.ds(pl.multiple_of(start, size), size)


class Attention:
    def __init__(self, core, ids, lens, kv, qs, gs, suf, score, prob, grad, dq):
        self.core, self.ids, self.lens = core, ids, lens
        self.kv, self.qs, self.gs, self.suf = kv, qs, gs, suf
        self.score, self.prob, self.grad, self.dq = score, prob, grad, dq

    def blocks(self, t, which, i):
        turn = self.core * TURNS + t
        return jnp.concatenate(
            [self.kv[which, self.ids[turn, i * GROUP + p], :, :] for p in range(GROUP)], 0
        )

    def own(self, t, which):
        return self.suf[aligned(t * TURN_LEN, TURN_LEN), which * HEAD_DIM:(which + 1) * HEAD_DIM]

    def rows(self, i):
        return aligned(i * STEP, STEP)

    def store_grad(self, t, i, value):
        for p in range(GROUP):
            self.grad[t, i * GROUP + p, :, :] = value[p * BLOCK:(p + 1) * BLOCK]

    def probabilities(self, t):
        score, prob, qs, gs = self.score, self.prob, self.qs, self.gs
        own = pl.ds(PICKED, TURN_LEN)
        length = self.lens[self.core * TURNS + t]
        s = dot(self.own(t, 0), qs[t], 1, 1)
        key_pos = lax.broadcasted_iota(jnp.int32, s.shape, 0)
        query_pos = lax.rem(lax.broadcasted_iota(jnp.int32, s.shape, 1), TURN_LEN)
        s = jnp.where((key_pos <= query_pos) & (key_pos < length), s, -1e30)
        score[own, :] = s

        def scores(i, top):
            s = dot(self.blocks(t, 0, i), qs[t], 1, 1)
            score[self.rows(i), :] = s
            return jnp.maximum(top, fold(s, jnp.max))

        top = lax.fori_loop(0, STEPS, scores, fold(s, jnp.max))
        top = jnp.max(top, axis=0, keepdims=True) * EXP_SCALE

        def exponential(where):
            e = jnp.exp2(score[where, :] * EXP_SCALE - top)
            score[where, :] = e
            return fold(e, jnp.sum)

        total = lax.fori_loop(
            0, STEPS, lambda i, total: total + exponential(self.rows(i)), exponential(own)
        )
        scale = 1.0 / jnp.sum(total, axis=0, keepdims=True)

        def value_grads(where):
            low = (score[where, :] * scale).astype(BF16)
            prob[t, where, :] = low
            return dot(low, gs[t], 1, 0)

        self.grad[t, PICKS, :, :] = value_grads(own)
        each(STEPS, lambda i: self.store_grad(t, i, value_grads(self.rows(i))))

    def score_grads(self, t, hook):
        gval, prob, qs, gs = self.score, self.prob, self.qs, self.gs
        own = pl.ds(PICKED, TURN_LEN)

        def products(where, value):
            v = dot(value, gs[t], 1, 1)
            gval[where, :] = v
            return fold(prob[t, where, :].astype(F32) * v, jnp.sum)

        def product_step(i, row_dot):
            row_dot = row_dot + products(self.rows(i), self.blocks(t, 1, i))
            hook(t * 2 * STEPS + i)
            return row_dot

        row_dot = lax.fori_loop(0, STEPS, product_step, products(own, self.own(t, 1)))
        row_dot = jnp.sum(row_dot, axis=0, keepdims=True)

        def key_grads(where):
            low = (prob[t, where, :].astype(F32) * (gval[where, :] - row_dot)).astype(BF16)
            prob[t, where, :] = low
            return dot(low, qs[t], 1, 0) * INV_ROOT

        self.grad[t, PICKS, :, :] = key_grads(own)

        def key_step(i):
            self.store_grad(t, i, key_grads(self.rows(i)))
            hook((t * 2 + 1) * STEPS + i)

        each(STEPS, key_step)

    def query_grads(self, t):
        self.dq[...] = dot(self.own(t, 0), self.prob[t, pl.ds(PICKED, TURN_LEN), :], 0, 0)

        def step(i):
            self.dq[...] += dot(self.blocks(t, 0, i), self.prob[t, self.rows(i), :], 0, 0)

        each(STEPS, step)


def kernel(
    ids, inv, lens, q_hbm, g_hbm, suf_hbm, kv_hbm, w_hbm,
    dq_hbm, dsuf_hbm, out_hbm,
    kv, q_own, q_peer, g_own, g_peer, qs, gs, suf, score, prob, grad, dq, dq_own, dq_peer, dsuf,
    send, acc, r_core, r_y0, r_z10, r_z20, r_z11, r_z21, r_y1, x,
    in_sems, s_in, s_out, out_sems, w_sems,
    s_core, s_y0, s_z10, s_z20, s_z11, s_z21, s_y1, s_t, s_g0, s_g1, s_own, ready,
):
    hs = lax.axis_index("hs")
    grp = lax.axis_index("grp")
    core, head = lax.rem(hs, 2), hs // 2
    y, z = grp // 4, lax.rem(grp, 4)
    zs = (lax.rem(z + 1, 4), lax.rem(z + 3, 4))
    zo = lax.rem(z + 2, 4)
    to_core = {"hs": head * 2 + 1 - core}
    to_y = {"grp": (1 - y) * 4 + z}
    to_z = [{"grp": y * 4 + zs[0]}, {"grp": y * 4 + zs[1]}]

    def copy_to(source, target, send_sem, recv_sem, device):
        return pltpu.make_async_remote_copy(
            source, target, send_sem, recv_sem, device_id=device, device_id_type=MESH
        )

    def remote(source, target, sems, index, device):
        return copy_to(source, target, sems.at[(0, *index)], sems.at[(1, *index)], device)

    barrier = pltpu.get_barrier_semaphore()

    def greet(semaphore, device):
        pl.semaphore_signal(semaphore, inc=1, device_id=device, device_id_type=MESH)

    neighbours = (to_core, to_y, *to_z)
    for device in neighbours:
        greet(barrier, device)
    for j in range(1, KV_HEADS):
        greet(barrier, {"hs": lax.rem(head + j, KV_HEADS) * 2 + core})

    def turns_of(c):
        return aligned(c * MINE, MINE)

    columns = aligned(head * 2 * HEAD_DIM, 2 * HEAD_DIM)
    local = [
        pltpu.make_async_copy(kv_hbm, kv.at[core], in_sems.at[0]),
        pltpu.make_async_copy(q_hbm.at[turns_of(core), :], q_own, in_sems.at[1]),
        pltpu.make_async_copy(g_hbm.at[turns_of(core), :], g_own, in_sems.at[2]),
        pltpu.make_async_copy(suf_hbm.at[turns_of(core), columns], suf, in_sems.at[3]),
    ]
    for copy in local:
        copy.start()
    pl.semaphore_wait(barrier, 3 + KV_HEADS)
    far = [
        remote(q_hbm.at[turns_of(1 - core), :], q_peer, s_in, (0,), to_core),
        remote(g_hbm.at[turns_of(1 - core), :], g_peer, s_in, (1,), to_core),
        remote(kv_hbm, kv.at[core], s_in, (2,), to_core),
    ]
    for copy in far:
        copy.start()
    for t in range(TURNS):
        grad[t, SLOTS, :, :] = jnp.zeros((BLOCK, HEAD_DIM), F32)
    for copy in local[1:]:
        copy.wait()
    for copy in far[:2]:
        copy.wait()

    def lanes(j):
        return slice(j % OWN_HEADS * HEAD_DIM, (j % OWN_HEADS + 1) * HEAD_DIM)

    def stack(t):
        where = aligned(t * TURN_LEN, TURN_LEN)
        live = lax.broadcasted_iota(jnp.int32, (TURN_LEN, HEAD_DIM), 0) < lens[core * TURNS + t]
        for j in range(2 * OWN_HEADS):
            q_from, g_from = (q_own, g_own) if j < OWN_HEADS else (q_peer, g_peer)
            here = slice(j * TURN_LEN, (j + 1) * TURN_LEN)
            qs[t, here, :] = q_from[where, lanes(j)]
            g = g_from[where, lanes(j)]
            gs[t, here, :] = jnp.where(live, g, jnp.zeros_like(g))

    each(TURNS, stack)
    local[0].wait()
    far[2].wait()

    def chunk_rows(part, count=1):
        return pl.ds(pl.multiple_of(part * CHUNK, CHUNK), count * CHUNK)

    def half_rows(part, d):
        return aligned(part * CHUNK + d * HALF, HALF)

    def core_copy(c):
        return remote(send.at[c], r_core.at[c], s_core, (c,), to_core)

    def y0(i):
        return remote(acc.at[i, chunk_rows((1 - y) * 4, 4), :], r_y0.at[i], s_y0, (i,), to_y)

    def z10(i, d):
        return remote(acc.at[i, half_rows(y * 4 + zo, d), :], r_z10.at[i, d], s_z10, (i, d), to_z[d])

    def z20(i, d):
        return remote(acc.at[i, chunk_rows(y * 4 + zs[d]), :], r_z20.at[i, d], s_z20, (i, d), to_z[d])

    def z11(i, d, v):
        return remote(
            acc.at[SET + i, half_rows(v * 4 + zo, d), :], r_z11.at[i, d, v], s_z11, (i, d, v), to_z[d]
        )

    def z21(i, d, v):
        return remote(
            acc.at[SET + i, chunk_rows(v * 4 + zs[d]), :], r_z21.at[i, d, v], s_z21, (i, d, v), to_z[d]
        )

    def y1(i):
        return remote(acc.at[SET + i, chunk_rows((1 - y) * 4 + z), :], r_y1.at[i], s_y1, (i,), to_y)

    def add(c, rows, *terms):
        total = acc[c, rows, :].astype(F32)
        for term in terms:
            total = total + term.astype(F32)
        acc[c, rows, :] = total.astype(BF16)

    def dense(target, c, k):
        for b in range(RANGE_BLOCKS):
            total = None
            for t in range(TURNS):
                slot = inv[core * TURNS + t, (c * 2 + k) * RANGE_BLOCKS + b]
                term = grad[t, slot, :, :]
                total = term if total is None else total + term
            target[c, b * BLOCK:(b + 1) * BLOCK, :] = total.astype(BF16)

    def send_core(i):
        for c in (i, SET + i):
            dense(send, c, 1 - core)
            core_copy(c).start()

    def keep_core(i):
        for c in (i, SET + i):
            dense(acc, c, core)

    def sum_cores(i):
        for c in (i, SET + i):
            core_copy(c).wait_recv()
            acc[c, :, :] = acc[c, :, :] + r_core[c, :, :]
        y0(i).start()
        for d in range(2):
            for v in range(2):
                z11(i, d, v).start()

    def z_second(i):
        for d in range(2):
            for v in range(2):
                z11(i, d, v).wait_recv()
                add(SET + i, half_rows(v * 4 + zs[d], d), r_z11[i, d, v])
        for d in range(2):
            for v in range(2):
                z21(i, d, v).start()

    def z_third(i):
        for d in range(2):
            for v in range(2):
                z21(i, d, v).wait_recv()
        for v in range(2):
            add(SET + i, chunk_rows(v * 4 + z), r_z21[i, 0, v], r_z21[i, 1, v])
        y1(i).start()

    def y_second(i):
        y0(i).wait_recv()
        add(i, chunk_rows(y * 4, 4), r_y0[i])
        for d in range(2):
            z10(i, d).start()

    def y_third(i):
        for d in range(2):
            z10(i, d).wait_recv()
            add(i, half_rows(y * 4 + zs[d], d), r_z10[i, d])
        for d in range(2):
            z20(i, d).start()

    def turn_out(f, c):
        return copy_to(
            acc.at[c, chunk_rows(grp), :], x.at[f, head, chunk_rows(grp), :],
            s_t.at[0, f, c], s_t.at[1, f, head], {"hs": c * 2 + core},
        )

    def turn_in(f, c):
        return copy_to(
            acc.at[c, chunk_rows(grp), :], x.at[f, c, chunk_rows(grp), :],
            s_t.at[0, f, c], s_t.at[1, f, c], {"hs": c * 2 + core},
        )

    def turn_own(f, c):
        return pltpu.make_async_copy(
            acc.at[c, chunk_rows(grp), :], x.at[f, c, chunk_rows(grp), :], s_own.at[f]
        )

    def hand_on(f, c):
        @pl.when(c != head)
        def _():
            turn_out(f, c).start()

        @pl.when(c == head)
        def _():
            turn_own(f, c).start()

    def y_fourth(f, i):
        for d in range(2):
            z20(i, d).wait_recv()
        add(i, chunk_rows(grp), r_z20[i, 0], r_z20[i, 1])
        hand_on(f, i)

    def z_fourth(f, i):
        y1(i).wait_recv()
        add(SET + i, chunk_rows(grp), r_y1[i])
        hand_on(f, SET + i)

    def sent_sets(f):
        def one(i):
            core_copy(i).wait_send()
            core_copy(SET + i).wait_send()
            y0(i).wait_send()
            y1(i).wait_send()
            for d in range(2):
                z10(i, d).wait_send()
                z20(i, d).wait_send()
                for v in range(2):
                    z11(i, d, v).wait_send()
                    z21(i, d, v).wait_send()

        def turned(c):
            @pl.when(c != head)
            def _():
                turn_out(f, c).wait_send()

        each(SET, one)
        each(KV_HEADS, turned)

    def part(v, place):
        return v * 4 + place

    def g_copy(f, sems, index, base, p, rows, device):
        where = x.at[f, pl.ds(base + p * PIECE, PIECE), rows, :]
        return remote(where, where, sems, (f, p, index), device)

    def gy0(f, p):
        return g_copy(f, s_g0, 0, 0, p, chunk_rows(grp), to_y)

    def gz10(f, p, d, far):
        return g_copy(f, s_g0, 1 + d + 2 * far, 0, p, chunk_rows(part(1 - y if far else y, z)), to_z[d])

    def gz20(f, p, d, far):
        rows = half_rows(part(1 - y if far else y, zs[1 - d]), d)
        return g_copy(f, s_g0, 5 + d + 2 * far, 0, p, rows, to_z[d])

    def gz11(f, p, d):
        return g_copy(f, s_g1, d, SET, p, chunk_rows(grp), to_z[d])

    def gz21(f, p, d):
        return g_copy(f, s_g1, 2 + d, SET, p, half_rows(part(y, zs[1 - d]), d), to_z[d])

    def gy1(f, p, which):
        place = (z, zs[0], zs[1], zo)[which]
        return g_copy(f, s_g1, 4 + which, SET, p, chunk_rows(part(y, place)), to_y)

    def arrived(f, c):
        @pl.when(c != head)
        def _():
            turn_in(f, c).wait_recv()

        @pl.when(c == head)
        def _():
            turn_own(f, c).wait()

    def gather_first(f, p):
        for j in range(PIECE):
            arrived(f, p * PIECE + j)
        gy0(f, p).start()
        for d in range(2):
            gz10(f, p, d, False).start()
        for j in range(PIECE):
            arrived(f, SET + p * PIECE + j)
        for d in range(2):
            gz11(f, p, d).start()
        gy1(f, p, 0).start()

    def gather_second(f, p):
        gy0(f, p).wait_recv()
        for d in range(2):
            gz10(f, p, d, True).start()
        for d in range(2):
            gz11(f, p, d).wait_recv()
            gy1(f, p, 2 - d).start()
            gz21(f, p, d).start()
        for d in range(2):
            gz10(f, p, d, False).wait_recv()
            gz20(f, p, d, False).start()

    def gather_third(f, p):
        for d in range(2):
            gz21(f, p, d).wait_recv()
        gy1(f, p, 3).start()
        for d in range(2):
            gz10(f, p, d, True).wait_recv()
            gz20(f, p, d, True).start()

    def gather_fourth(f, p):
        for d in range(2):
            gz20(f, p, d, False).wait_recv()
            gz20(f, p, d, True).wait_recv()
        for which in range(4):
            gy1(f, p, which).wait_recv()

    def sent_gather(f, p):
        gy0(f, p).wait_send()
        for d in range(2):
            gz11(f, p, d).wait_send()
            gz21(f, p, d).wait_send()
            for far in (False, True):
                gz10(f, p, d, far).wait_send()
                gz20(f, p, d, far).wait_send()
        for which in range(4):
            gy1(f, p, which).wait_send()

    def w_copy(f, c):
        source = aligned(c * 2 * HEAD_DIM + (1 - f) * HEAD_DIM, HEAD_DIM)
        return pltpu.make_async_copy(
            w_hbm.at[:, source],
            prob.at[0, aligned(f * RANGE, RANGE), aligned(c * HEAD_DIM, HEAD_DIM)],
            w_sems.at[f, c],
        )

    def out_copy(rows, index):
        return pltpu.make_async_copy(prob.at[1, rows, :], out_hbm.at[rows, :], out_sems.at[index])

    def product(f, rows):
        left = jnp.concatenate([x[f, c, rows, :] for c in range(KV_HEADS)], 1)
        return dot(left, prob[0, f * RANGE:(f + 1) * RANGE, :], 1, 1)

    def value_product(i):
        rows = aligned(i * 2 * CHUNK, 2 * CHUNK)
        score[rows, :] = product(0, rows)

    def key_product(rows, index):
        prob[1, rows, :] = (score[rows, :] + product(1, rows)).astype(BF16)
        out_copy(rows, index).start()

    work = Attention(core, ids, lens, kv, qs, gs, suf, score, prob, grad, dq)
    each(TURNS, work.probabilities)
    each(SET, send_core)

    def keep_value(t):
        dsuf[1, aligned(t * TURN_LEN, TURN_LEN), :] = grad[t, PICKS, :, :].astype(BF16)

    each(TURNS, keep_value)
    each(SET, keep_core)

    def release():
        for device in neighbours:
            greet(ready, device)

    plan = {
        1: [lambda: sum_cores(0), lambda: sum_cores(1)],
        2: [lambda: sum_cores(2), lambda: sum_cores(3)],
        3: [lambda: each(SET, z_second)],
        4: [lambda: y_second(0)],
        5: [lambda: z_third(0), lambda: z_third(1)],
        6: [lambda: y_second(1), lambda: y_third(0)],
        7: [lambda: z_third(2), lambda: z_third(3)],
        8: [lambda: y_fourth(0, 0)],
        9: [lambda: y_second(2), lambda: y_third(1)],
        10: [lambda: y_fourth(0, 1)],
        11: [lambda: y_second(3), lambda: y_third(2)],
        12: [lambda: y_fourth(0, 2)],
        13: [lambda: y_third(3), lambda: z_fourth(0, 0), lambda: z_fourth(0, 1)],
        14: [lambda: y_fourth(0, 3), lambda: z_fourth(0, 2)],
        15: [lambda: z_fourth(0, 3), release],
    }

    def hook(n):
        for at, steps in plan.items():
            @pl.when(n == at)
            def _(steps=steps):
                for step in steps:
                    step()

    each(TURNS, lambda t: work.score_grads(t, hook))

    sent_sets(0)
    pl.semaphore_wait(ready, len(neighbours))
    each(SET, send_core)
    each(PIECES, lambda p: gather_first(0, p))

    def keep_key(t):
        dsuf[0, aligned(t * TURN_LEN, TURN_LEN), :] = grad[t, PICKS, :, :].astype(BF16)

    each(TURNS, keep_key)
    each(SET, keep_core)
    each(SET, sum_cores)

    def query_out(t):
        work.query_grads(t)
        where = aligned(t * TURN_LEN, TURN_LEN)
        for j in range(2 * OWN_HEADS):
            target = dq_own if j < OWN_HEADS else dq_peer
            part_t = dq[:, j * TURN_LEN:(j + 1) * TURN_LEN] * INV_ROOT
            target[where, lanes(j)] = part_t.T.astype(BF16)

    query_out(0)
    each(2, lambda f: each(KV_HEADS, lambda c: w_copy(f, c).start()))
    each(PIECES, lambda p: gather_second(0, p))
    each(SET, z_second)
    y_second(0)
    query_out(1)
    results = [
        pltpu.make_async_copy(dq_own, dq_hbm.at[turns_of(core), :], in_sems.at[0]),
        pltpu.make_async_copy(dsuf.at[core], dsuf_hbm.at[turns_of(core), :], in_sems.at[1]),
        remote(dq_peer, dq_hbm.at[turns_of(core), :], s_out, (0,), to_core),
        remote(dsuf.at[1 - core], dsuf_hbm.at[turns_of(core), :], s_out, (1,), to_core),
    ]
    for copy in results:
        copy.start()
    each(PIECES, lambda p: gather_third(0, p))
    y_third(0)
    y_second(1)
    z_third(0)
    z_third(1)
    y_fourth(1, 0)
    y_third(1)
    z_third(2)
    z_third(3)
    y_second(2)
    each(PIECES, lambda p: gather_fourth(0, p))
    y_fourth(1, 1)
    y_third(2)
    each(2, lambda f: each(KV_HEADS, lambda c: w_copy(f, c).wait()))
    each(2, value_product)
    y_fourth(1, 2)
    y_second(3)
    y_third(3)
    z_fourth(1, 0)
    each(2, lambda i: value_product(2 + i))
    z_fourth(1, 1)
    y_fourth(1, 3)
    z_fourth(1, 2)
    z_fourth(1, 3)

    each(PIECES, lambda p: gather_first(1, p))
    each(PIECES, lambda p: gather_second(1, p))
    key_product(chunk_rows(grp), 0)
    each(PIECES, lambda p: gather_third(1, p))
    key_product(chunk_rows(part(y, zs[0])), 1)
    key_product(chunk_rows(part(y, zs[1])), 2)
    each(PIECES, lambda p: gather_fourth(1, p))
    key_product(chunk_rows(part(y, zo)), 3)
    for v in range(2):
        key_product(chunk_rows(part(1 - y, 2 * v), 2), 4 + v)

    for copy in results:
        copy.wait()
    sent_sets(1)
    for f in range(2):
        each(PIECES, lambda p, f=f: sent_gather(f, p))
    for index, place in enumerate((part(y, z), part(y, zs[0]), part(y, zs[1]), part(y, zo))):
        out_copy(chunk_rows(place), index).wait()
    for v in range(2):
        out_copy(chunk_rows(part(1 - y, 2 * v), 2), 4 + v).wait()


def fused(ids, inv, lens, q, g, suf, kv, weight):
    width = OWN_HEADS * HEAD_DIM
    dma = pltpu.SemaphoreType.DMA
    scratch = [
        pltpu.VMEM((2, PREFIX_BLOCKS, BLOCK, HEAD_DIM), BF16),
        pltpu.VMEM((MINE, width), BF16),
        pltpu.VMEM((MINE, width), BF16),
        pltpu.VMEM((MINE, width), BF16),
        pltpu.VMEM((MINE, width), BF16),
        pltpu.VMEM((TURNS, ROWS, HEAD_DIM), BF16),
        pltpu.VMEM((TURNS, ROWS, HEAD_DIM), BF16),
        pltpu.VMEM((MINE, 2 * HEAD_DIM), BF16),
        pltpu.VMEM((KEYS, ROWS), F32),
        pltpu.VMEM((TURNS, KEYS, ROWS), BF16),
        pltpu.VMEM((TURNS, SLOTS + 1, BLOCK, HEAD_DIM), F32),
        pltpu.VMEM((HEAD_DIM, ROWS), F32),
        pltpu.VMEM((MINE, width), BF16),
        pltpu.VMEM((MINE, width), BF16),
        pltpu.VMEM((2, MINE, HEAD_DIM), BF16),
        pltpu.VMEM((KV_HEADS, RANGE, HEAD_DIM), BF16),
        pltpu.VMEM((KV_HEADS, RANGE, HEAD_DIM), BF16),
        pltpu.VMEM((KV_HEADS, RANGE, HEAD_DIM), BF16),
        pltpu.VMEM((SET, 4 * CHUNK, HEAD_DIM), BF16),
        pltpu.VMEM((SET, 2, HALF, HEAD_DIM), BF16),
        pltpu.VMEM((SET, 2, CHUNK, HEAD_DIM), BF16),
        pltpu.VMEM((SET, 2, 2, HALF, HEAD_DIM), BF16),
        pltpu.VMEM((SET, 2, 2, CHUNK, HEAD_DIM), BF16),
        pltpu.VMEM((SET, CHUNK, HEAD_DIM), BF16),
        pltpu.VMEM((2, KV_HEADS, RANGE, HEAD_DIM), BF16),
        dma((4,)),
        dma((2, 3)),
        dma((2, 2)),
        dma((6,)),
        dma((2, KV_HEADS)),
        dma((2, KV_HEADS)),
        dma((2, SET)),
        dma((2, SET, 2)),
        dma((2, SET, 2)),
        dma((2, SET, 2, 2)),
        dma((2, SET, 2, 2)),
        dma((2, SET)),
        dma((2, 2, KV_HEADS)),
        dma((2, 2, PIECES, 9)),
        dma((2, 2, PIECES, 8)),
        dma((2,)),
        pltpu.SemaphoreType.REGULAR,
    ]
    return pl.pallas_call(
        kernel,
        out_shape=[
            jax.ShapeDtypeStruct((2 * MINE, width), BF16),
            jax.ShapeDtypeStruct((2 * MINE, HEAD_DIM), BF16),
            jax.ShapeDtypeStruct((RANGE, weight.shape[0]), BF16),
        ],
        in_specs=[SMEM, SMEM, SMEM, HBM, HBM, HBM, HBM, HBM],
        out_specs=[HBM, HBM, HBM],
        scratch_shapes=scratch,
        compiler_params=pltpu.CompilerParams(
            collective_id=0, has_side_effects=True, vmem_limit_bytes=64 * MIB
        ),
        name="attention_backward",
    )(ids, inv, lens, q, g, suf, kv.reshape(PREFIX_BLOCKS, BLOCK, HEAD_DIM), weight)


def on_device(queries, d_out, suffix_kv, prefix_kv, kv_weight, block_ids, lengths):
    blocks = jnp.arange(PREFIX_BLOCKS, dtype=jnp.int32)
    picks = jnp.arange(PICKS, dtype=jnp.int32) - SLOTS
    named = block_ids[:, :, None] == blocks
    inverse = jnp.sum(jnp.where(named, picks[None, :, None], 0), axis=1) + SLOTS
    return tuple(
        fused(block_ids, inverse, lengths, queries, d_out, suffix_kv, prefix_kv, kv_weight)
    )


def solution(mesh):
    placed = (
        P("grp", "hs"),
        P("grp", "hs"),
        P("grp", None),
        P(None, "hs"),
        P("grp", None),
        P("grp", None),
        P("grp"),
    )
    return jax.shard_map(
        on_device,
        mesh=mesh,
        in_specs=placed,
        out_specs=(P("grp", "hs"), P("grp", "hs"), P("hs", "grp")),
        check_vma=False,
    )
```

```python
import functools
import math

import jax
import jax.numpy as jnp
from jax import lax
from jax.experimental import pallas as pl
from jax.experimental.pallas import tpu as pltpu
from jax.sharding import PartitionSpec as P

KV_HEADS = 8
HEAD_DIM = 128
BLOCK = 128
PICKS = 32
TURN_LEN = 128
PREFIX = 16384
PREFIX_BLOCKS = 128

OWN_HEADS = 4
TURNS = 2
MINE = TURNS * TURN_LEN
ROWS = 2 * OWN_HEADS * TURN_LEN
PICKED = PICKS * BLOCK
KEYS = PICKED + TURN_LEN
SLOTS = PICKS + 1
STEPS = 3
GROUP = SLOTS // STEPS
STEP = GROUP * BLOCK
PREFIX_STEP = STEP - TURN_LEN
INV_ROOT = 1.0 / math.sqrt(HEAD_DIM)
EXP_SCALE = INV_ROOT * math.log2(math.e)
RANGE = PREFIX // (2 * KV_HEADS)
RANGE_BLOCKS = RANGE // BLOCK
PARTS = 8
CHUNK = RANGE // PARTS
HALF = CHUNK // 2
YSET = 3
ZSET = KV_HEADS - YSET
SET = KV_HEADS // 2
PIECES = 2
PIECE = SET // PIECES
COPIES = 4
F32 = jnp.float32
BF16 = jnp.bfloat16
MIB = 1 << 20
MESH = pl.DeviceIdType.MESH
HBM = pl.BlockSpec(memory_space=pl.ANY)
SMEM = pl.BlockSpec(memory_space=pltpu.SMEM)


def dot(a, b, ca, cb):
    return lax.dot_general(a, b, (((ca,), (cb,)), ((), ())), preferred_element_type=F32)


def fold(x, op):
    return op(x.reshape(x.shape[0] // 8, 8, x.shape[1]), axis=0)


def each(count, body):
    def step(i, carry):
        body(i)
        return carry

    lax.fori_loop(0, count, step, 0)


def aligned(start, size):
    return pl.ds(pl.multiple_of(start, size), size)


class Attention:
    def __init__(self, core, ids, lens, kv, qs, gs, score, prob, grad, dq):
        self.core, self.ids, self.lens = core, ids, lens
        self.kv, self.qs, self.gs = kv, qs, gs
        self.score, self.prob, self.grad, self.dq = score, prob, grad, dq

    def blocks(self, t, which, i):
        turn = self.core * TURNS + t
        parts = []
        for p in range(GROUP):
            slot = i * GROUP + p
            if p < GROUP - 1:
                index = self.ids[turn, slot]
            else:
                index = jnp.where(
                    slot < PICKS, self.ids[turn, jnp.minimum(slot, PICKS - 1)], PREFIX_BLOCKS + t
                )
            parts.append(self.kv[which, index, :, :])
        return jnp.concatenate(parts, 0)

    def rows(self, i):
        return aligned(i * STEP, STEP)

    def store_grad(self, t, i, value):
        for p in range(GROUP):
            self.grad[t, i * GROUP + p, :, :] = value[p * BLOCK:(p + 1) * BLOCK]

    def probabilities(self, t):
        score, prob, qs, gs = self.score, self.prob, self.qs, self.gs
        length = self.lens[self.core * TURNS + t]
        shape = (TURN_LEN, ROWS)
        key_pos = lax.broadcasted_iota(jnp.int32, shape, 0)
        query_pos = lax.rem(lax.broadcasted_iota(jnp.int32, shape, 1), TURN_LEN)
        own_allowed = (key_pos <= query_pos) & (key_pos < length)

        def scores(i, top):
            s = dot(self.blocks(t, 0, i), qs[t], 1, 1)
            own = jnp.where(own_allowed | (i < STEPS - 1), s[PREFIX_STEP:], -1e30)
            s = jnp.concatenate([s[:PREFIX_STEP], own], 0)
            score[self.rows(i), :] = s
            return jnp.maximum(top, fold(s, jnp.max))

        top = lax.fori_loop(0, STEPS, scores, jnp.full((8, ROWS), -1e30, F32))
        top = jnp.max(top, axis=0, keepdims=True) * EXP_SCALE

        def exponentials(i, total):
            e = jnp.exp2(score[self.rows(i), :] * EXP_SCALE - top)
            score[self.rows(i), :] = e
            return total + fold(e, jnp.sum)

        total = lax.fori_loop(0, STEPS, exponentials, jnp.zeros((8, ROWS), F32))
        scale = 1.0 / jnp.sum(total, axis=0, keepdims=True)

        def value_grads(i):
            low = (score[self.rows(i), :] * scale).astype(BF16)
            prob[t, self.rows(i), :] = low
            self.store_grad(t, i, dot(low, gs[t], 1, 0))

        each(STEPS, value_grads)

    def score_grads(self, t, hook):
        gval, prob, qs, gs = self.score, self.prob, self.qs, self.gs

        def products(i, row_dot):
            v = dot(self.blocks(t, 1, i), gs[t], 1, 1)
            gval[self.rows(i), :] = v
            row_dot = row_dot + fold(prob[t, self.rows(i), :].astype(F32) * v, jnp.sum)
            hook(t * 2 * STEPS + i)
            return row_dot

        row_dot = lax.fori_loop(0, STEPS, products, jnp.zeros((8, ROWS), F32))
        row_dot = jnp.sum(row_dot, axis=0, keepdims=True)

        def key_grads(i):
            rows = self.rows(i)
            low = (prob[t, rows, :].astype(F32) * (gval[rows, :] - row_dot)).astype(BF16)
            prob[t, rows, :] = low
            self.store_grad(t, i, dot(low, qs[t], 1, 0) * INV_ROOT)
            hook((t * 2 + 1) * STEPS + i)

        each(STEPS, key_grads)

    def query_grads(self, t):
        self.dq[...] = jnp.zeros_like(self.dq)

        def step(i):
            self.dq[...] += dot(self.blocks(t, 0, i), self.prob[t, self.rows(i), :], 0, 0)

        each(STEPS, step)


def kernel(
    ids, inv, lens, q_hbm, g_hbm, suf_hbm, kv_hbm, w_hbm,
    dq_hbm, dsuf_hbm, out_hbm,
    kv, q_own, q_peer, g_own, g_peer, qs, gs, suf, score, prob, grad, dq, dq_own, dq_peer, dsuf,
    send, acc, r_core, r_y0, r_z10, r_z20, r_z11, r_z21, r_y1, x,
    in_sems, s_in, s_out, out_sems, w_sems,
    s_core, s_y0, s_z10, s_z20, s_z11, s_z21, s_y1, s_t, s_g0, s_g1, s_own, ready,
):
    hs = lax.axis_index("hs")
    grp = lax.axis_index("grp")
    core, head = lax.rem(hs, 2), hs // 2
    y, z = grp // 4, lax.rem(grp, 4)
    zs = (lax.rem(z + 1, 4), lax.rem(z + 3, 4))
    zo = lax.rem(z + 2, 4)
    to_core = {"hs": head * 2 + 1 - core}
    to_y = {"grp": (1 - y) * 4 + z}
    to_z = [{"grp": y * 4 + zs[0]}, {"grp": y * 4 + zs[1]}]

    def copy_to(source, target, send_sem, recv_sem, device):
        return pltpu.make_async_remote_copy(
            source, target, send_sem, recv_sem, device_id=device, device_id_type=MESH
        )

    def remote(source, target, sems, index, device):
        return copy_to(source, target, sems.at[(0, *index)], sems.at[(1, *index)], device)

    barrier = pltpu.get_barrier_semaphore()

    def greet(semaphore, device):
        pl.semaphore_signal(semaphore, inc=1, device_id=device, device_id_type=MESH)

    neighbours = (to_core, to_y, *to_z)
    for device in neighbours:
        greet(barrier, device)
    for j in range(1, KV_HEADS):
        greet(barrier, {"hs": lax.rem(head + j, KV_HEADS) * 2 + core})

    def turns_of(c):
        return aligned(c * MINE, MINE)

    columns = aligned(head * 2 * HEAD_DIM, 2 * HEAD_DIM)
    local = [
        pltpu.make_async_copy(kv_hbm, kv.at[core, pl.ds(0, PREFIX_BLOCKS)], in_sems.at[0]),
        pltpu.make_async_copy(q_hbm.at[turns_of(core), :], q_own, in_sems.at[1]),
        pltpu.make_async_copy(g_hbm.at[turns_of(core), :], g_own, in_sems.at[2]),
        pltpu.make_async_copy(suf_hbm.at[turns_of(core), columns], suf, in_sems.at[3]),
    ]
    for copy in local:
        copy.start()
    pl.semaphore_wait(barrier, 3 + KV_HEADS)
    far = [
        remote(q_hbm.at[turns_of(1 - core), :], q_peer, s_in, (0,), to_core),
        remote(g_hbm.at[turns_of(1 - core), :], g_peer, s_in, (1,), to_core),
    ]
    for j in range(COPIES):
        some = pl.ds(j * PREFIX_BLOCKS // COPIES, PREFIX_BLOCKS // COPIES)
        far.append(remote(kv_hbm.at[some], kv.at[core, some], s_in, (2 + j,), to_core))
    for copy in far:
        copy.start()
    for t in range(TURNS):
        grad[t, SLOTS, :, :] = jnp.zeros((BLOCK, HEAD_DIM), F32)
    for copy in local[1:]:
        copy.wait()
    for copy in far[:2]:
        copy.wait()

    def lanes(j):
        return slice(j % OWN_HEADS * HEAD_DIM, (j % OWN_HEADS + 1) * HEAD_DIM)

    def stack(t):
        where = aligned(t * TURN_LEN, TURN_LEN)
        live = lax.broadcasted_iota(jnp.int32, (TURN_LEN, HEAD_DIM), 0) < lens[core * TURNS + t]
        for j in range(2 * OWN_HEADS):
            q_from, g_from = (q_own, g_own) if j < OWN_HEADS else (q_peer, g_peer)
            here = slice(j * TURN_LEN, (j + 1) * TURN_LEN)
            qs[t, here, :] = q_from[where, lanes(j)]
            g = g_from[where, lanes(j)]
            gs[t, here, :] = jnp.where(live, g, jnp.zeros_like(g))

    each(TURNS, stack)
    for t in range(TURNS):
        for which in range(2):
            own = suf[t * TURN_LEN:(t + 1) * TURN_LEN, which * HEAD_DIM:(which + 1) * HEAD_DIM]
            kv[which, PREFIX_BLOCKS + t, :, :] = own
    local[0].wait()
    for copy in far[2:]:
        copy.wait()

    def chunk_rows(part, count=1):
        return pl.ds(pl.multiple_of(part * CHUNK, CHUNK), count * CHUNK)

    def half_rows(part, d):
        return aligned(part * CHUNK + d * HALF, HALF)

    def core_copy(c):
        return remote(send.at[c], r_core.at[c], s_core, (c,), to_core)

    def y0(i):
        return remote(acc.at[i, chunk_rows((1 - y) * 4, 4), :], r_y0.at[i], s_y0, (i,), to_y)

    def z10(i, d):
        return remote(acc.at[i, half_rows(y * 4 + zo, d), :], r_z10.at[i, d], s_z10, (i, d), to_z[d])

    def z20(i, d):
        return remote(acc.at[i, chunk_rows(y * 4 + zs[d]), :], r_z20.at[i, d], s_z20, (i, d), to_z[d])

    def z11(i, d, v):
        return remote(
            acc.at[YSET + i, half_rows(v * 4 + zo, d), :], r_z11.at[i, d, v], s_z11, (i, d, v), to_z[d]
        )

    def z21(i, d, v):
        return remote(
            acc.at[YSET + i, chunk_rows(v * 4 + zs[d]), :], r_z21.at[i, d, v], s_z21, (i, d, v), to_z[d]
        )

    def y1(i):
        return remote(acc.at[YSET + i, chunk_rows((1 - y) * 4 + z), :], r_y1.at[i], s_y1, (i,), to_y)

    def add(c, rows, *terms):
        total = acc[c, rows, :].astype(F32)
        for term in terms:
            total = total + term.astype(F32)
        acc[c, rows, :] = total.astype(BF16)

    def dense(c, k, b):
        total = None
        for t in range(TURNS):
            slot = inv[core * TURNS + t, (c * 2 + k) * RANGE_BLOCKS + b]
            term = grad[t, slot, :, :]
            total = term if total is None else total + term
        return total

    def send_core(c):
        for b in range(RANGE_BLOCKS):
            send[c, b * BLOCK:(b + 1) * BLOCK, :] = dense(c, 1 - core, b).astype(BF16)
        core_copy(c).start()

    def sum_core(c):
        core_copy(c).wait_recv()
        for b in range(RANGE_BLOCKS):
            rows = slice(b * BLOCK, (b + 1) * BLOCK)
            acc[c, rows, :] = (dense(c, core, b) + r_core[c, rows, :].astype(F32)).astype(BF16)

    def y_first(i):
        sum_core(i)
        y0(i).start()

    def z_first(i):
        sum_core(YSET + i)
        for d in range(2):
            for v in range(2):
                z11(i, d, v).start()

    def z_second(i):
        for d in range(2):
            for v in range(2):
                z11(i, d, v).wait_recv()
                add(YSET + i, half_rows(v * 4 + zs[d], d), r_z11[i, d, v])
        for d in range(2):
            for v in range(2):
                z21(i, d, v).start()

    def z_third(i):
        for d in range(2):
            for v in range(2):
                z21(i, d, v).wait_recv()
        for v in range(2):
            add(YSET + i, chunk_rows(v * 4 + z), r_z21[i, 0, v], r_z21[i, 1, v])
        y1(i).start()

    def y_second(i):
        y0(i).wait_recv()
        add(i, chunk_rows(y * 4, 4), r_y0[i])
        for d in range(2):
            z10(i, d).start()

    def y_third(i):
        for d in range(2):
            z10(i, d).wait_recv()
            add(i, half_rows(y * 4 + zs[d], d), r_z10[i, d])
        for d in range(2):
            z20(i, d).start()

    def turn_out(f, c):
        return copy_to(
            acc.at[c, chunk_rows(grp), :], x.at[f, head, chunk_rows(grp), :],
            s_t.at[0, f, c], s_t.at[1, f, head], {"hs": c * 2 + core},
        )

    def turn_in(f, c):
        return copy_to(
            acc.at[c, chunk_rows(grp), :], x.at[f, c, chunk_rows(grp), :],
            s_t.at[0, f, c], s_t.at[1, f, c], {"hs": c * 2 + core},
        )

    def turn_own(f, c):
        return pltpu.make_async_copy(
            acc.at[c, chunk_rows(grp), :], x.at[f, c, chunk_rows(grp), :], s_own.at[f]
        )

    def hand_on(f, c):
        @pl.when(c != head)
        def _():
            turn_out(f, c).start()

        @pl.when(c == head)
        def _():
            turn_own(f, c).start()

    def y_fourth(f, i):
        for d in range(2):
            z20(i, d).wait_recv()
        add(i, chunk_rows(grp), r_z20[i, 0], r_z20[i, 1])
        hand_on(f, i)

    def z_fourth(f, i):
        y1(i).wait_recv()
        add(YSET + i, chunk_rows(grp), r_y1[i])
        hand_on(f, YSET + i)

    def sent_sets(f):
        def sent_y(i):
            y0(i).wait_send()
            for d in range(2):
                z10(i, d).wait_send()
                z20(i, d).wait_send()

        def sent_z(i):
            y1(i).wait_send()
            for d in range(2):
                for v in range(2):
                    z11(i, d, v).wait_send()
                    z21(i, d, v).wait_send()

        def turned(c):
            @pl.when(c != head)
            def _():
                turn_out(f, c).wait_send()

        each(KV_HEADS, lambda c: core_copy(c).wait_send())
        each(YSET, sent_y)
        each(ZSET, sent_z)
        each(KV_HEADS, turned)

    def part(v, place):
        return v * 4 + place

    def g_copy(f, sems, index, base, p, rows, device):
        where = x.at[f, pl.ds(base + p * PIECE, PIECE), rows, :]
        return remote(where, where, sems, (f, p, index), device)

    def gy0(f, p):
        return g_copy(f, s_g0, 0, 0, p, chunk_rows(grp), to_y)

    def gz10(f, p, d, far):
        return g_copy(f, s_g0, 1 + d + 2 * far, 0, p, chunk_rows(part(1 - y if far else y, z)), to_z[d])

    def gz20(f, p, d, far):
        rows = half_rows(part(1 - y if far else y, zs[1 - d]), d)
        return g_copy(f, s_g0, 5 + d + 2 * far, 0, p, rows, to_z[d])

    def gz11(f, p, d):
        return g_copy(f, s_g1, d, SET, p, chunk_rows(grp), to_z[d])

    def gz21(f, p, d):
        return g_copy(f, s_g1, 2 + d, SET, p, half_rows(part(y, zs[1 - d]), d), to_z[d])

    def gy1(f, p, which):
        place = (z, zs[0], zs[1], zo)[which]
        return g_copy(f, s_g1, 4 + which, SET, p, chunk_rows(part(y, place)), to_y)

    def arrived(f, c):
        @pl.when(c != head)
        def _():
            turn_in(f, c).wait_recv()

        @pl.when(c == head)
        def _():
            turn_own(f, c).wait()

    def gather_first(f, p):
        for j in range(PIECE):
            arrived(f, p * PIECE + j)
        gy0(f, p).start()
        for d in range(2):
            gz10(f, p, d, False).start()
        for j in range(PIECE):
            arrived(f, SET + p * PIECE + j)
        for d in range(2):
            gz11(f, p, d).start()
        gy1(f, p, 0).start()

    def gather_second(f, p):
        gy0(f, p).wait_recv()
        for d in range(2):
            gz10(f, p, d, True).start()
        for d in range(2):
            gz11(f, p, d).wait_recv()
            gy1(f, p, 2 - d).start()
            gz21(f, p, d).start()
        for d in range(2):
            gz10(f, p, d, False).wait_recv()
            gz20(f, p, d, False).start()

    def gather_third(f, p):
        for d in range(2):
            gz21(f, p, d).wait_recv()
        gy1(f, p, 3).start()
        for d in range(2):
            gz10(f, p, d, True).wait_recv()
            gz20(f, p, d, True).start()

    def gather_fourth(f, p):
        for d in range(2):
            gz20(f, p, d, False).wait_recv()
            gz20(f, p, d, True).wait_recv()
        for which in range(1 if f else 0, 4):
            gy1(f, p, which).wait_recv()

    def sent_gather(f, p):
        gy0(f, p).wait_send()
        for d in range(2):
            gz11(f, p, d).wait_send()
            gz21(f, p, d).wait_send()
            for far in (False, True):
                gz10(f, p, d, far).wait_send()
                gz20(f, p, d, far).wait_send()
        for which in range(4):
            gy1(f, p, which).wait_send()

    def w_copy(f, c):
        source = aligned(c * 2 * HEAD_DIM + (1 - f) * HEAD_DIM, HEAD_DIM)
        return pltpu.make_async_copy(
            w_hbm.at[:, source],
            prob.at[0, aligned(f * RANGE, RANGE), aligned(c * HEAD_DIM, HEAD_DIM)],
            w_sems.at[f, c],
        )

    def out_copy(place):
        rows = chunk_rows(place)
        return pltpu.make_async_copy(prob.at[1, rows, :], out_hbm.at[rows, :], out_sems.at[place])

    def product(f, places):
        left = jnp.concatenate(
            [
                jnp.concatenate([x[f, c, chunk_rows(place), :] for c in range(KV_HEADS)], 1)
                for place in places
            ],
            0,
        )
        return dot(left, prob[0, f * RANGE:(f + 1) * RANGE, :], 1, 1)

    def value_product(i):
        places = (2 * i, 2 * i + 1)
        score[aligned(i * 2 * CHUNK, 2 * CHUNK), :] = product(0, places)

    def key_product(*places):
        result = product(1, places)
        for j, place in enumerate(places):
            rows = chunk_rows(place)
            total = score[rows, :] + result[j * CHUNK:(j + 1) * CHUNK]
            prob[1, rows, :] = total.astype(BF16)
            out_copy(place).start()

    work = Attention(core, ids, lens, kv, qs, gs, score, prob, grad, dq)
    each(TURNS, work.probabilities)
    each(KV_HEADS, send_core)

    def keep_value(t):
        dsuf[1, aligned(t * TURN_LEN, TURN_LEN), :] = grad[t, PICKS, :, :].astype(BF16)

    each(TURNS, keep_value)

    def release():
        for device in neighbours:
            greet(ready, device)

    plan = {
        0: [],
        1: [lambda: y_second(0), lambda: each(2, z_second)],
        2: [lambda: each(3, lambda i: z_second(2 + i)), lambda: y_second(1), lambda: y_third(0)],
        3: [lambda: y_second(2), lambda: z_third(0)],
        4: [lambda: each(2, lambda i: z_third(1 + i)), lambda: y_third(1)],
        5: [lambda: each(2, lambda i: z_third(3 + i)), lambda: y_fourth(0, 0), lambda: y_third(2)],
        6: [lambda: each(3, lambda i: z_fourth(0, i)), lambda: y_fourth(0, 1)],
        7: [lambda: each(2, lambda i: z_fourth(0, 3 + i)), lambda: y_fourth(0, 2), release],
        9: [lambda: each(PIECES, lambda p: gather_first(0, p))],
        11: [lambda: each(PIECES, lambda p: gather_second(0, p))],
    }

    def hook(n):
        for at, steps in plan.items():
            @pl.when(n == at)
            def _(steps=steps):
                for step in steps:
                    step()

    each(YSET, y_first)
    each(ZSET, z_first)
    each(TURNS, lambda t: work.score_grads(t, hook))

    sent_sets(0)
    pl.semaphore_wait(ready, len(neighbours))
    each(KV_HEADS, send_core)

    def keep_key(t):
        dsuf[0, aligned(t * TURN_LEN, TURN_LEN), :] = grad[t, PICKS, :, :].astype(BF16)

    each(TURNS, keep_key)
    each(YSET, y_first)
    each(ZSET, z_first)
    each(PIECES, lambda p: gather_third(0, p))

    def query_out(t):
        work.query_grads(t)
        where = aligned(t * TURN_LEN, TURN_LEN)
        for j in range(2 * OWN_HEADS):
            target = dq_own if j < OWN_HEADS else dq_peer
            part_t = dq[:, j * TURN_LEN:(j + 1) * TURN_LEN] * INV_ROOT
            target[where, lanes(j)] = part_t.T.astype(BF16)

    y_second(0)
    each(2, z_second)
    query_out(0)
    each(2, lambda f: each(KV_HEADS, lambda c: w_copy(f, c).start()))
    y_second(1)
    each(3, lambda i: z_second(2 + i))
    y_third(0)
    query_out(1)
    results = [
        pltpu.make_async_copy(dq_own, dq_hbm.at[turns_of(core), :], in_sems.at[0]),
        pltpu.make_async_copy(dsuf.at[core], dsuf_hbm.at[turns_of(core), :], in_sems.at[1]),
        remote(dq_peer, dq_hbm.at[turns_of(core), :], s_out, (0,), to_core),
        remote(dsuf.at[1 - core], dsuf_hbm.at[turns_of(core), :], s_out, (1,), to_core),
    ]
    for copy in results:
        copy.start()
    y_second(2)
    z_third(0)
    each(2, lambda f: each(KV_HEADS, lambda c: w_copy(f, c).wait()))
    y_third(1)
    each(PIECES, lambda p: gather_fourth(0, p))
    each(2, value_product)
    each(2, lambda i: z_third(1 + i))
    y_third(2)
    each(2, lambda i: z_third(3 + i))
    y_fourth(1, 0)
    each(2, lambda i: value_product(2 + i))
    each(2, lambda i: z_fourth(1, i))
    y_fourth(1, 1)
    each(2, lambda i: z_fourth(1, 2 + i))
    y_fourth(1, 2)
    z_fourth(1, 4)

    each(PIECES, lambda p: gather_first(1, p))
    each(PIECES, lambda p: gather_second(1, p))
    each(PIECES, lambda p: gy1(1, p, 0).wait_recv())
    key_product(part(y, z), part(1 - y, z))
    each(PIECES, lambda p: gather_third(1, p))
    key_product(part(y, zs[0]), part(y, zs[1]))
    each(PIECES, lambda p: gather_fourth(1, p))
    key_product(part(1 - y, zs[0]), part(1 - y, zs[1]))
    key_product(part(y, zo), part(1 - y, zo))

    for copy in results:
        copy.wait()
    sent_sets(1)
    for f in range(2):
        each(PIECES, lambda p, f=f: sent_gather(f, p))
    each(PARTS, lambda place: out_copy(place).wait())


def copy_kernel(*refs):
    count = (len(refs) - 2) // 3
    sources, targets, rooms = (refs[i * count:(i + 1) * count] for i in range(3))
    in_sems, out_sems = refs[-2:]

    def parts(make):
        index = 0
        for source, target, room in zip(sources, targets, rooms):
            rows = source.shape[0] // COPIES
            for j in range(COPIES):
                make(index, source, target, room, pl.ds(j * rows, rows))
                index += 1

    def read(index, source, target, room, where):
        return pltpu.make_async_copy(source.at[where, :], room.at[where, :], in_sems.at[index])

    def write(index, source, target, room, where):
        return pltpu.make_async_copy(room.at[where, :], target.at[where, :], out_sems.at[index])

    def pass_on(*args):
        read(*args).wait()
        write(*args).start()

    parts(lambda *args: read(*args).start())
    parts(pass_on)
    parts(lambda *args: write(*args).wait())


def separate(arrays):
    hbm = pl.BlockSpec(memory_space=pltpu.HBM)
    pieces = COPIES * len(arrays)
    return pl.pallas_call(
        copy_kernel,
        out_shape=[jax.ShapeDtypeStruct(array.shape, array.dtype) for array in arrays],
        in_specs=[hbm] * len(arrays),
        out_specs=[hbm] * len(arrays),
        scratch_shapes=[
            *(pltpu.VMEM(array.shape, array.dtype) for array in arrays),
            pltpu.SemaphoreType.DMA((pieces,)),
            pltpu.SemaphoreType.DMA((pieces,)),
        ],
        compiler_params=pltpu.CompilerParams(vmem_limit_bytes=64 * MIB),
        name="separate",
    )(*arrays)


def fused(ids, inv, lens, q, g, suf, kv, weight):
    width = OWN_HEADS * HEAD_DIM
    dma = pltpu.SemaphoreType.DMA
    scratch = [
        pltpu.VMEM((2, PREFIX_BLOCKS + TURNS, BLOCK, HEAD_DIM), BF16),
        pltpu.VMEM((MINE, width), BF16),
        pltpu.VMEM((MINE, width), BF16),
        pltpu.VMEM((MINE, width), BF16),
        pltpu.VMEM((MINE, width), BF16),
        pltpu.VMEM((TURNS, ROWS, HEAD_DIM), BF16),
        pltpu.VMEM((TURNS, ROWS, HEAD_DIM), BF16),
        pltpu.VMEM((MINE, 2 * HEAD_DIM), BF16),
        pltpu.VMEM((KEYS, ROWS), F32),
        pltpu.VMEM((TURNS, KEYS, ROWS), BF16),
        pltpu.VMEM((TURNS, SLOTS + 1, BLOCK, HEAD_DIM), F32),
        pltpu.VMEM((HEAD_DIM, ROWS), F32),
        pltpu.VMEM((MINE, width), BF16),
        pltpu.VMEM((MINE, width), BF16),
        pltpu.VMEM((2, MINE, HEAD_DIM), BF16),
        pltpu.VMEM((KV_HEADS, RANGE, HEAD_DIM), BF16),
        pltpu.VMEM((KV_HEADS, RANGE, HEAD_DIM), BF16),
        pltpu.VMEM((KV_HEADS, RANGE, HEAD_DIM), BF16),
        pltpu.VMEM((YSET, 4 * CHUNK, HEAD_DIM), BF16),
        pltpu.VMEM((YSET, 2, HALF, HEAD_DIM), BF16),
        pltpu.VMEM((YSET, 2, CHUNK, HEAD_DIM), BF16),
        pltpu.VMEM((ZSET, 2, 2, HALF, HEAD_DIM), BF16),
        pltpu.VMEM((ZSET, 2, 2, CHUNK, HEAD_DIM), BF16),
        pltpu.VMEM((ZSET, CHUNK, HEAD_DIM), BF16),
        pltpu.VMEM((2, KV_HEADS, RANGE, HEAD_DIM), BF16),
        dma((4,)),
        dma((2, 2 + COPIES)),
        dma((2, 2)),
        dma((PARTS,)),
        dma((2, KV_HEADS)),
        dma((2, KV_HEADS)),
        dma((2, YSET)),
        dma((2, YSET, 2)),
        dma((2, YSET, 2)),
        dma((2, ZSET, 2, 2)),
        dma((2, ZSET, 2, 2)),
        dma((2, ZSET)),
        dma((2, 2, KV_HEADS)),
        dma((2, 2, PIECES, 9)),
        dma((2, 2, PIECES, 8)),
        dma((2,)),
        pltpu.SemaphoreType.REGULAR,
    ]
    return pl.pallas_call(
        kernel,
        out_shape=[
            jax.ShapeDtypeStruct((2 * MINE, width), BF16),
            jax.ShapeDtypeStruct((2 * MINE, HEAD_DIM), BF16),
            jax.ShapeDtypeStruct((RANGE, weight.shape[0]), BF16),
        ],
        in_specs=[SMEM, SMEM, SMEM, HBM, HBM, HBM, HBM, HBM],
        out_specs=[HBM, HBM, HBM],
        scratch_shapes=scratch,
        compiler_params=pltpu.CompilerParams(
            collective_id=0, has_side_effects=True, vmem_limit_bytes=64 * MIB
        ),
        name="attention_backward",
    )(ids, inv, lens, q, g, suf, kv.reshape(PREFIX_BLOCKS, BLOCK, HEAD_DIM), weight)


def on_device(queries, d_out, suffix_kv, prefix_kv, kv_weight, block_ids, lengths):
    blocks = jnp.arange(PREFIX_BLOCKS, dtype=jnp.int32)
    picks = jnp.arange(PICKS, dtype=jnp.int32)
    named = block_ids[:, :, None] == blocks
    inverse = jnp.min(jnp.where(named, picks[None, :, None], SLOTS), axis=1)
    return tuple(
        separate(
            fused(block_ids, inverse, lengths, queries, d_out, suffix_kv, prefix_kv, kv_weight)
        )
    )


def solution(mesh):
    placed = (
        P("grp", "hs"),
        P("grp", "hs"),
        P("grp", None),
        P(None, "hs"),
        P("grp", None),
        P("grp", None),
        P("grp"),
    )
    return jax.shard_map(
        on_device,
        mesh=mesh,
        in_specs=placed,
        out_specs=(P("grp", "hs"), P("grp", "hs"), P("hs", "grp")),
        check_vma=False,
    )
```

```python
import functools
import math

import jax
import jax.numpy as jnp
from jax import lax
from jax.experimental import pallas as pl
from jax.experimental.pallas import tpu as pltpu
from jax.sharding import PartitionSpec as P

KV_HEADS = 8
HEAD_DIM = 128
BLOCK = 128
PICKS = 32
TURN_LEN = 128
PREFIX = 16384
PREFIX_BLOCKS = 128

OWN_HEADS = 4
TURNS = 2
MINE = TURNS * TURN_LEN
ROWS = 2 * OWN_HEADS * TURN_LEN
PICKED = PICKS * BLOCK
KEYS = PICKED + TURN_LEN
SLOTS = PICKS + 1
STEPS = 3
GROUP = SLOTS // STEPS
STEP = GROUP * BLOCK
PREFIX_STEP = STEP - TURN_LEN
INV_ROOT = 1.0 / math.sqrt(HEAD_DIM)
EXP_SCALE = INV_ROOT * math.log2(math.e)
RANGE = PREFIX // (2 * KV_HEADS)
RANGE_BLOCKS = RANGE // BLOCK
PARTS = 8
CHUNK = RANGE // PARTS
SETS = ((0, 3), (3, 3), (6, 2))
ORDERS = ((0, 1, 2), (1, 2, 0), (2, 0, 1))
REDUCE_TURN = (0, 2)
GATHER_TURN = (1, 0)


def turned_on(order, turn):
    return tuple((d + turn) % 3 for d in order)


COPIES = 4
F32 = jnp.float32
BF16 = jnp.bfloat16
MIB = 1 << 20
MESH = pl.DeviceIdType.MESH
HBM = pl.BlockSpec(memory_space=pl.ANY)
SMEM = pl.BlockSpec(memory_space=pltpu.SMEM)


def dot(a, b, ca, cb):
    return lax.dot_general(a, b, (((ca,), (cb,)), ((), ())), preferred_element_type=F32)


def fold(x, op):
    return op(x.reshape(x.shape[0] // 8, 8, x.shape[1]), axis=0)


def each(count, body):
    def step(i, carry):
        body(i)
        return carry

    lax.fori_loop(0, count, step, 0)


def aligned(start, size):
    return pl.ds(pl.multiple_of(start, size), size)


class Attention:
    def __init__(self, core, ids, lens, kv, qs, gs, score, prob, grad, dq):
        self.core, self.ids, self.lens = core, ids, lens
        self.kv, self.qs, self.gs = kv, qs, gs
        self.score, self.prob, self.grad, self.dq = score, prob, grad, dq

    def blocks(self, t, which, i):
        turn = self.core * TURNS + t
        parts = []
        for p in range(GROUP):
            slot = i * GROUP + p
            if p < GROUP - 1:
                index = self.ids[turn, slot]
            else:
                index = jnp.where(
                    slot < PICKS, self.ids[turn, jnp.minimum(slot, PICKS - 1)], PREFIX_BLOCKS + t
                )
            parts.append(self.kv[which, index, :, :])
        return jnp.concatenate(parts, 0)

    def rows(self, i):
        return aligned(i * STEP, STEP)

    def store_grad(self, t, i, value):
        for p in range(GROUP):
            self.grad[t, i * GROUP + p, :, :] = value[p * BLOCK:(p + 1) * BLOCK]

    def scores(self, t):
        length = self.lens[self.core * TURNS + t]
        shape = (TURN_LEN, ROWS)
        key_pos = lax.broadcasted_iota(jnp.int32, shape, 0)
        query_pos = lax.rem(lax.broadcasted_iota(jnp.int32, shape, 1), TURN_LEN)
        own_allowed = (key_pos <= query_pos) & (key_pos < length)

        def step(i, top):
            s = dot(self.blocks(t, 0, i), self.qs[t], 1, 1)
            own = jnp.where(own_allowed | (i < STEPS - 1), s[PREFIX_STEP:], -1e30)
            s = jnp.concatenate([s[:PREFIX_STEP], own], 0)
            self.score[self.rows(i), :] = s
            return jnp.maximum(top, fold(s, jnp.max))

        return step

    def exponentials(self, top):
        top = jnp.max(top, axis=0, keepdims=True) * EXP_SCALE

        def step(i, total):
            e = jnp.exp2(self.score[self.rows(i), :] * EXP_SCALE - top)
            self.score[self.rows(i), :] = e
            return total + fold(e, jnp.sum)

        total = lax.fori_loop(0, STEPS, step, jnp.zeros((8, ROWS), F32))
        return 1.0 / jnp.sum(total, axis=0, keepdims=True)

    def value_grads(self, t, scale, i):
        low = (self.score[self.rows(i), :] * scale).astype(BF16)
        self.prob[t, self.rows(i), :] = low
        self.store_grad(t, i, dot(low, self.gs[t], 1, 0))

    def probabilities(self):
        least = jnp.full((8, ROWS), -1e30, F32)
        scale = self.exponentials(lax.fori_loop(0, STEPS, self.scores(0), least))
        scores = self.scores(1)

        def step(i, top):
            self.value_grads(0, scale, i)
            return scores(i, top)

        scale_1 = self.exponentials(lax.fori_loop(0, STEPS, step, least))
        each(STEPS, lambda i: self.value_grads(1, scale_1, i))

    def score_grads(self, t, hook):
        gval, prob, qs, gs = self.score, self.prob, self.qs, self.gs

        def products(i, row_dot):
            v = dot(self.blocks(t, 1, i), gs[t], 1, 1)
            gval[self.rows(i), :] = v
            row_dot = row_dot + fold(prob[t, self.rows(i), :].astype(F32) * v, jnp.sum)
            hook(t * 2 * STEPS + i)
            return row_dot

        row_dot = lax.fori_loop(0, STEPS, products, jnp.zeros((8, ROWS), F32))
        row_dot = jnp.sum(row_dot, axis=0, keepdims=True)

        def key_grads(i):
            rows = self.rows(i)
            low = (prob[t, rows, :].astype(F32) * (gval[rows, :] - row_dot)).astype(BF16)
            prob[t, rows, :] = low
            self.store_grad(t, i, dot(low, qs[t], 1, 0) * INV_ROOT)
            hook((t * 2 + 1) * STEPS + i)

        each(STEPS, key_grads)

    def query_grads(self, t):
        self.dq[...] = jnp.zeros_like(self.dq)

        def step(i):
            self.dq[...] += dot(self.blocks(t, 0, i), self.prob[t, self.rows(i), :], 0, 0)

        each(STEPS, step)


def kernel(
    ids, inv, lens, q_hbm, g_hbm, suf_hbm, kv_hbm, w_hbm,
    dq_hbm, dsuf_hbm, out_hbm,
    kv, q_own, q_peer, g_own, g_peer, qs, gs, suf, score, prob, grad, dq, dsuf,
    send, acc, r_first, r_second, r_third, x,
    in_sems, s_in, s_out, out_sems, w_sems,
    s_core, s_legs, s_t, s_hops, s_own,
):
    hs = lax.axis_index("hs")
    grp = lax.axis_index("grp")
    core, head = lax.rem(hs, 2), hs // 2
    y, z = grp // 4, lax.rem(grp, 4)
    here = (y, lax.rem((z + 1) // 2, 2), z // 2)
    to_core = {"hs": head * 2 + 1 - core}
    along = (
        {"grp": (1 - y) * 4 + z},
        {"grp": y * 4 + z + 1 - 2 * lax.rem(z, 2)},
        {"grp": y * 4 + 3 - z},
    )

    def copy_to(source, target, send_sem, recv_sem, device):
        return pltpu.make_async_remote_copy(
            source, target, send_sem, recv_sem, device_id=device, device_id_type=MESH
        )

    def remote(source, target, sems, index, device):
        return copy_to(source, target, sems.at[(0, *index)], sems.at[(1, *index)], device)

    barrier = pltpu.get_barrier_semaphore()

    def greet(semaphore, device):
        pl.semaphore_signal(semaphore, inc=1, device_id=device, device_id_type=MESH)

    neighbours = (to_core, *along)
    for device in neighbours:
        greet(barrier, device)
    for j in range(1, KV_HEADS):
        greet(barrier, {"hs": lax.rem(head + j, KV_HEADS) * 2 + core})

    def turns_of(c):
        return aligned(c * MINE, MINE)

    columns = aligned(head * 2 * HEAD_DIM, 2 * HEAD_DIM)
    local = [
        pltpu.make_async_copy(kv_hbm, kv.at[core, pl.ds(0, PREFIX_BLOCKS)], in_sems.at[0]),
        pltpu.make_async_copy(q_hbm.at[turns_of(core), :], q_own, in_sems.at[1]),
        pltpu.make_async_copy(g_hbm.at[turns_of(core), :], g_own, in_sems.at[2]),
        pltpu.make_async_copy(suf_hbm.at[turns_of(core), columns], suf, in_sems.at[3]),
    ]
    for copy in local:
        copy.start()
    pl.semaphore_wait(barrier, 3 + KV_HEADS)
    far = [
        remote(q_hbm.at[turns_of(1 - core), :], q_peer, s_in, (0,), to_core),
        remote(g_hbm.at[turns_of(1 - core), :], g_peer, s_in, (1,), to_core),
    ]
    for j in range(COPIES):
        some = pl.ds(j * PREFIX_BLOCKS // COPIES, PREFIX_BLOCKS // COPIES)
        far.append(remote(kv_hbm.at[some], kv.at[core, some], s_in, (2 + j,), to_core))
    for copy in far:
        copy.start()
    for t in range(TURNS):
        grad[t, SLOTS, :, :] = jnp.zeros((BLOCK, HEAD_DIM), F32)
    for copy in local[1:]:
        copy.wait()
    for copy in far[:2]:
        copy.wait()

    def lanes(j):
        return slice(j % OWN_HEADS * HEAD_DIM, (j % OWN_HEADS + 1) * HEAD_DIM)

    def stack(t):
        where = aligned(t * TURN_LEN, TURN_LEN)
        live = lax.broadcasted_iota(jnp.int32, (TURN_LEN, HEAD_DIM), 0) < lens[core * TURNS + t]
        for j in range(2 * OWN_HEADS):
            q_from, g_from = (q_own, g_own) if j < OWN_HEADS else (q_peer, g_peer)
            here = slice(j * TURN_LEN, (j + 1) * TURN_LEN)
            qs[t, here, :] = q_from[where, lanes(j)]
            g = g_from[where, lanes(j)]
            gs[t, here, :] = jnp.where(live, g, jnp.zeros_like(g))

    each(TURNS, stack)
    for t in range(TURNS):
        for which in range(2):
            own = suf[t * TURN_LEN:(t + 1) * TURN_LEN, which * HEAD_DIM:(which + 1) * HEAD_DIM]
            kv[which, PREFIX_BLOCKS + t, :, :] = own
    local[0].wait()
    for copy in far[2:]:
        copy.wait()

    def core_copy(f, c):
        return remote(send.at[c], acc.at[f, c], s_core, (f, c), to_core)

    def at(**fixed):
        return tuple(fixed.get(name, slice(None)) for name in ("d0", "d1", "d2"))

    def cube(directions, flip=()):
        return at(**{f"d{d}": 1 - here[d] if d in flip else here[d] for d in directions})

    landing = (r_first, r_second, r_third)

    def leg(f, c, order, step):
        index = cube(order[:step + 1], order[step:step + 1])
        return remote(
            acc.at[(f, c, *index)], landing[step].at[f, c], s_legs, (f, step, c), along[order[step]]
        )

    def leg_in(f, c, order, step):
        leg(f, c, order, step).wait_recv()
        index = (f, c, *cube(order[:step + 1]))
        total = acc[index].astype(F32) + landing[step][f, c].astype(F32)
        acc[index] = total.astype(BF16)

    def corner(b):
        return b // 4, b // 2 % 2, b % 2

    def dense(c, k, b):
        total = None
        for t in range(TURNS):
            slot = inv[core * TURNS + t, (c * 2 + k) * RANGE_BLOCKS + b]
            term = grad[t, slot, :, :]
            total = term if total is None else total + term
        return total

    def send_core(f, c):
        for b in range(RANGE_BLOCKS):
            send[(c, *corner(b))] = dense(c, 1 - core, b).astype(BF16)
        core_copy(f, c).start()

    def sum_core(f, c):
        core_copy(f, c).wait_recv()
        for b in range(RANGE_BLOCKS):
            where = (f, c, *corner(b))
            acc[where] = (dense(c, core, b) + acc[where].astype(F32)).astype(BF16)

    def turn_out(f, c):
        return copy_to(
            acc.at[(f, c, *here)], x.at[(f, head, *here)],
            s_t.at[0, f, c], s_t.at[1, f, head], {"hs": c * 2 + core},
        )

    def turn_in(f, c):
        return copy_to(
            acc.at[(f, c, *here)], x.at[(f, c, *here)],
            s_t.at[0, f, c], s_t.at[1, f, c], {"hs": c * 2 + core},
        )

    def turn_own(f, c):
        return pltpu.make_async_copy(acc.at[(f, c, *here)], x.at[(f, c, *here)], s_own.at[f])

    def hand_on(f, c):
        @pl.when(c != head)
        def _():
            turn_out(f, c).start()

        @pl.when(c == head)
        def _():
            turn_own(f, c).start()

    def reduce_order(f, which):
        return turned_on(ORDERS[which], REDUCE_TURN[f])

    def first(which, i, f):
        c = SETS[which][0] + i
        sum_core(f, c)
        leg(f, c, reduce_order(f, which), 0).start()

    def later(which, i, f, step):
        c = SETS[which][0] + i
        leg_in(f, c, reduce_order(f, which), step - 1)
        leg(f, c, reduce_order(f, which), step).start()

    def last(which, i, f):
        c = SETS[which][0] + i
        leg_in(f, c, reduce_order(f, which), 2)
        hand_on(f, c)

    def row(i, step, *args):
        for which in range(len(SETS)):
            if i < SETS[which][1]:
                step(which, i, *args)

    def sent_core(f):
        each(KV_HEADS, lambda c: core_copy(f, c).wait_send())

    def sent_sets(f):
        def turned(c):
            @pl.when(c != head)
            def _():
                turn_out(f, c).wait_send()

        for which, (base, count) in enumerate(SETS):
            for step in range(3):
                each(count, lambda i: leg(f, base + i, reduce_order(f, which), step).wait_send())
        each(KV_HEADS, turned)

    def arrived(f, c):
        @pl.when(c != head)
        def _():
            turn_in(f, c).wait_recv()

        @pl.when(c == head)
        def _():
            turn_own(f, c).wait()

    PATHS = (((), 0), ((), 1), ((), 2), ((0,), 1), ((0,), 2), ((1,), 2), ((0, 1), 2))

    def hop(f, which, path):
        base, count = SETS[which]
        order = turned_on(ORDERS[which][::-1], GATHER_TURN[f])
        crossed, following = PATHS[path]
        index = cube((0, 1, 2), tuple(order[d] for d in crossed))
        block = x.at[(f, pl.ds(base, count), *index)]
        return remote(block, block, s_hops, (f, which, path), along[order[following]])

    def gather_first(f):
        for which, (base, count) in enumerate(SETS):
            each(count, lambda i: arrived(f, base + i))
            hop(f, which, 0).start()
        for path in (1, 2):
            for which in range(len(SETS)):
                hop(f, which, path).start()

    def gather_second(f):
        for which in range(len(SETS)):
            hop(f, which, 0).wait_recv()
            hop(f, which, 3).start()
            hop(f, which, 4).start()

    def gather_third(f):
        for which in range(len(SETS)):
            hop(f, which, 1).wait_recv()
            hop(f, which, 5).start()

    def gather_fourth(f):
        for which in range(len(SETS)):
            hop(f, which, 3).wait_recv()
            hop(f, which, 6).start()

    def gather_wait(f, *paths):
        for path in paths:
            for which in range(len(SETS)):
                hop(f, which, path).wait_recv()

    def sent_gather(f):
        for which in range(len(SETS)):
            for path in range(len(PATHS)):
                hop(f, which, path).wait_send()

    def w_copy(f, c):
        source = aligned(c * 2 * HEAD_DIM + (1 - f) * HEAD_DIM, HEAD_DIM)
        return pltpu.make_async_copy(
            w_hbm.at[:, source],
            prob.at[0, aligned(f * RANGE, RANGE), aligned(c * HEAD_DIM, HEAD_DIM)],
            w_sems.at[f, c],
        )

    def out_copy(place):
        rows = aligned((place[0] * 4 + place[1] * 2 + place[2]) * CHUNK, CHUNK)
        sem = out_sems.at[place[0] * 4 + place[1] * 2 + place[2]]
        return pltpu.make_async_copy(prob.at[1, rows, :], out_hbm.at[rows, :], sem)

    def product(f, places):
        left = jnp.concatenate(
            [
                jnp.concatenate([x[(f, c, *place)] for c in range(KV_HEADS)], 1)
                for place in places
            ],
            0,
        )
        return dot(left, prob[0, f * RANGE:(f + 1) * RANGE, :], 1, 1)

    def value_product(i):
        places = [(i // 2, lax.rem(i, 2), b) for b in range(2)]
        score[aligned(i * 2 * CHUNK, 2 * CHUNK), :] = product(0, places)

    def key_product(*flips):
        places = [cube((0, 1, 2), flip) for flip in flips]
        result = product(1, places)
        for j, place in enumerate(places):
            rows = aligned((place[0] * 4 + place[1] * 2 + place[2]) * CHUNK, CHUNK)
            total = score[rows, :] + result[j * CHUNK:(j + 1) * CHUNK]
            prob[1, rows, :] = total.astype(BF16)
            out_copy(place).start()

    work = Attention(core, ids, lens, kv, qs, gs, score, prob, grad, dq)
    work.probabilities()
    each(KV_HEADS, lambda c: send_core(0, c))

    def keep_value(t):
        dsuf[1, aligned(t * TURN_LEN, TURN_LEN), :] = grad[t, PICKS, :, :].astype(BF16)

    each(TURNS, keep_value)

    def firsts(f):
        def pair(i):
            for which in range(len(SETS)):
                first(which, i, f)

        each(2, pair)
        row(2, first, f)

    plan = {
        3: [lambda: row(0, later, 0, 1)],
        6: [lambda: row(1, later, 0, 1)],
        8: [lambda: row(2, later, 0, 1)],
        9: [lambda: row(0, later, 0, 2)],
        11: [lambda: row(1, later, 0, 2)],
    }

    def hook(n):
        for at, steps in plan.items():
            @pl.when(n == at)
            def _(steps=steps):
                for step in steps:
                    step()

    firsts(0)
    each(TURNS, lambda t: work.score_grads(t, hook))

    sent_core(0)
    each(KV_HEADS, lambda c: send_core(1, c))

    def keep_key(t):
        dsuf[0, aligned(t * TURN_LEN, TURN_LEN), :] = grad[t, PICKS, :, :].astype(BF16)

    each(TURNS, keep_key)
    row(2, later, 0, 2)
    row(0, last, 0)
    firsts(1)
    row(1, last, 0)
    row(2, last, 0)

    def query_out(t):
        work.query_grads(t)
        where = aligned(t * TURN_LEN, TURN_LEN)
        for j in range(2 * OWN_HEADS):
            target = q_own if j < OWN_HEADS else g_own
            part_t = dq[:, j * TURN_LEN:(j + 1) * TURN_LEN] * INV_ROOT
            target[where, lanes(j)] = part_t.T.astype(BF16)

    query_out(0)
    each(2, lambda f: each(KV_HEADS, lambda c: w_copy(f, c).start()))
    row(0, later, 1, 1)
    gather_first(0)
    query_out(1)
    results = [
        pltpu.make_async_copy(q_own, dq_hbm.at[turns_of(core), :], in_sems.at[0]),
        pltpu.make_async_copy(dsuf.at[core], dsuf_hbm.at[turns_of(core), :], in_sems.at[1]),
        remote(g_own, dq_hbm.at[turns_of(core), :], s_out, (0,), to_core),
        remote(dsuf.at[1 - core], dsuf_hbm.at[turns_of(core), :], s_out, (1,), to_core),
    ]
    for copy in results:
        copy.start()
    row(1, later, 1, 1)
    row(2, later, 1, 1)
    gather_second(0)
    row(0, later, 1, 2)
    gather_third(0)
    row(1, later, 1, 2)
    gather_fourth(0)
    row(2, later, 1, 2)
    row(0, last, 1)
    each(2, lambda f: each(KV_HEADS, lambda c: w_copy(f, c).wait()))
    row(1, last, 1)
    row(2, last, 1)
    gather_wait(0, 2, 4, 5, 6)
    each(4, value_product)

    gather_first(1)
    sent_core(1)
    sent_sets(0)
    gather_second(1)
    gather_third(1)
    gather_wait(1, 2)
    key_product((), (0,))
    gather_fourth(1)
    key_product((1,), (2,))
    sent_sets(1)
    sent_gather(0)
    for copy in results:
        copy.wait()
    gather_wait(1, 4, 5)
    key_product((0, 1), (0, 2))
    gather_wait(1, 6)
    key_product((1, 2), (0, 1, 2))

    sent_gather(1)
    each(PARTS, lambda i: out_copy((i // 4, lax.rem(i // 2, 2), lax.rem(i, 2))).wait())


def copy_kernel(*refs):
    count = (len(refs) - 2) // 3
    sources, targets, rooms = (refs[i * count:(i + 1) * count] for i in range(3))
    in_sems, out_sems = refs[-2:]

    def parts(make):
        index = 0
        for source, target, room in zip(sources, targets, rooms):
            rows = source.shape[0] // COPIES
            for j in range(COPIES):
                make(index, source, target, room, pl.ds(j * rows, rows))
                index += 1

    def read(index, source, target, room, where):
        return pltpu.make_async_copy(source.at[where, :], room.at[where, :], in_sems.at[index])

    def write(index, source, target, room, where):
        return pltpu.make_async_copy(room.at[where, :], target.at[where, :], out_sems.at[index])

    def pass_on(*args):
        read(*args).wait()
        write(*args).start()

    parts(lambda *args: read(*args).start())
    parts(pass_on)
    parts(lambda *args: write(*args).wait())


def separate(arrays):
    hbm = pl.BlockSpec(memory_space=pltpu.HBM)
    pieces = COPIES * len(arrays)
    return pl.pallas_call(
        copy_kernel,
        out_shape=[jax.ShapeDtypeStruct(array.shape, array.dtype) for array in arrays],
        in_specs=[hbm] * len(arrays),
        out_specs=[hbm] * len(arrays),
        scratch_shapes=[
            *(pltpu.VMEM(array.shape, array.dtype) for array in arrays),
            pltpu.SemaphoreType.DMA((pieces,)),
            pltpu.SemaphoreType.DMA((pieces,)),
        ],
        compiler_params=pltpu.CompilerParams(vmem_limit_bytes=64 * MIB),
        name="separate",
    )(*arrays)


def fused(ids, inv, lens, q, g, suf, kv, weight):
    width = OWN_HEADS * HEAD_DIM
    dma = pltpu.SemaphoreType.DMA
    scratch = [
        pltpu.VMEM((2, PREFIX_BLOCKS + TURNS, BLOCK, HEAD_DIM), BF16),
        pltpu.VMEM((MINE, width), BF16),
        pltpu.VMEM((MINE, width), BF16),
        pltpu.VMEM((MINE, width), BF16),
        pltpu.VMEM((MINE, width), BF16),
        pltpu.VMEM((TURNS, ROWS, HEAD_DIM), BF16),
        pltpu.VMEM((TURNS, ROWS, HEAD_DIM), BF16),
        pltpu.VMEM((MINE, 2 * HEAD_DIM), BF16),
        pltpu.VMEM((KEYS, ROWS), F32),
        pltpu.VMEM((TURNS, KEYS, ROWS), BF16),
        pltpu.VMEM((TURNS, SLOTS + 1, BLOCK, HEAD_DIM), F32),
        pltpu.VMEM((HEAD_DIM, ROWS), F32),
        pltpu.VMEM((2, MINE, HEAD_DIM), BF16),
        pltpu.VMEM((KV_HEADS, 2, 2, 2, CHUNK, HEAD_DIM), BF16),
        pltpu.VMEM((2, KV_HEADS, 2, 2, 2, CHUNK, HEAD_DIM), BF16),
        pltpu.VMEM((2, KV_HEADS, 2, 2, CHUNK, HEAD_DIM), BF16),
        pltpu.VMEM((2, KV_HEADS, 2, CHUNK, HEAD_DIM), BF16),
        pltpu.VMEM((2, KV_HEADS, CHUNK, HEAD_DIM), BF16),
        pltpu.VMEM((2, KV_HEADS, 2, 2, 2, CHUNK, HEAD_DIM), BF16),
        dma((4,)),
        dma((2, 2 + COPIES)),
        dma((2, 2)),
        dma((PARTS,)),
        dma((2, KV_HEADS)),
        dma((2, 2, KV_HEADS)),
        dma((2, 2, 3, KV_HEADS)),
        dma((2, 2, KV_HEADS)),
        dma((2, 2, len(SETS), 7)),
        dma((2,)),
    ]
    return pl.pallas_call(
        kernel,
        out_shape=[
            jax.ShapeDtypeStruct((2 * MINE, width), BF16),
            jax.ShapeDtypeStruct((2 * MINE, HEAD_DIM), BF16),
            jax.ShapeDtypeStruct((RANGE, weight.shape[0]), BF16),
        ],
        in_specs=[SMEM, SMEM, SMEM, HBM, HBM, HBM, HBM, HBM],
        out_specs=[HBM, HBM, HBM],
        scratch_shapes=scratch,
        compiler_params=pltpu.CompilerParams(
            collective_id=0, has_side_effects=True, vmem_limit_bytes=64 * MIB
        ),
        name="attention_backward",
    )(ids, inv, lens, q, g, suf, kv.reshape(PREFIX_BLOCKS, BLOCK, HEAD_DIM), weight)


def on_device(queries, d_out, suffix_kv, prefix_kv, kv_weight, block_ids, lengths):
    blocks = jnp.arange(PREFIX_BLOCKS, dtype=jnp.int32)
    picks = jnp.arange(PICKS, dtype=jnp.int32)
    named = block_ids[:, :, None] == blocks
    inverse = jnp.min(jnp.where(named, picks[None, :, None], SLOTS), axis=1)
    return tuple(
        separate(
            fused(block_ids, inverse, lengths, queries, d_out, suffix_kv, prefix_kv, kv_weight)
        )
    )


def solution(mesh):
    placed = (
        P("grp", "hs"),
        P("grp", "hs"),
        P("grp", None),
        P(None, "hs"),
        P("grp", None),
        P("grp", None),
        P("grp"),
    )
    return jax.shard_map(
        on_device,
        mesh=mesh,
        in_specs=placed,
        out_specs=(P("grp", "hs"), P("grp", "hs"), P("hs", "grp")),
        check_vma=False,
    )
```

```python
import functools
import math

import jax
import jax.numpy as jnp
from jax import lax
from jax.experimental import pallas as pl
from jax.experimental.pallas import tpu as pltpu
from jax.sharding import PartitionSpec as P

KV_HEADS = 8
HEAD_DIM = 128
BLOCK = 128
PICKS = 32
TURN_LEN = 128
PREFIX = 16384
PREFIX_BLOCKS = 128

OWN_HEADS = 4
TURNS = 2
MINE = TURNS * TURN_LEN
ROWS = 2 * OWN_HEADS * TURN_LEN
PICKED = PICKS * BLOCK
KEYS = PICKED + TURN_LEN
SLOTS = PICKS + 1
STEPS = 3
GROUP = SLOTS // STEPS
STEP = GROUP * BLOCK
PREFIX_STEP = STEP - TURN_LEN
INV_ROOT = 1.0 / math.sqrt(HEAD_DIM)
EXP_SCALE = INV_ROOT * math.log2(math.e)
RANGE = PREFIX // (2 * KV_HEADS)
RANGE_BLOCKS = RANGE // BLOCK
PARTS = 8
CHUNK = RANGE // PARTS
SETS = ((0, 3), (3, 3), (6, 2))
ORDERS = ((0, 1, 2), (1, 2, 0), (2, 0, 1))
REDUCE_TURN = (0, 2)
GATHER_TURN = (1, 0)


def turned_on(order, turn):
    return tuple((d + turn) % 3 for d in order)


COPIES = 4
F32 = jnp.float32
BF16 = jnp.bfloat16
MIB = 1 << 20
MESH = pl.DeviceIdType.MESH
HBM = pl.BlockSpec(memory_space=pl.ANY)
SMEM = pl.BlockSpec(memory_space=pltpu.SMEM)


def dot(a, b, ca, cb):
    return lax.dot_general(a, b, (((ca,), (cb,)), ((), ())), preferred_element_type=F32)


def fold(x, op):
    return op(x.reshape(x.shape[0] // 8, 8, x.shape[1]), axis=0)


def each(count, body):
    def step(i, carry):
        body(i)
        return carry

    lax.fori_loop(0, count, step, 0)


def aligned(start, size):
    return pl.ds(pl.multiple_of(start, size), size)


class Attention:
    def __init__(self, core, ids, lens, kv, qs, gs, score, prob, grad, dq):
        self.core, self.ids, self.lens = core, ids, lens
        self.kv, self.qs, self.gs = kv, qs, gs
        self.score, self.prob, self.grad, self.dq = score, prob, grad, dq

    def blocks(self, t, which, i):
        turn = self.core * TURNS + t
        parts = []
        for p in range(GROUP):
            slot = i * GROUP + p
            if p < GROUP - 1:
                index = self.ids[turn, slot]
            else:
                index = jnp.where(
                    slot < PICKS, self.ids[turn, jnp.minimum(slot, PICKS - 1)], PREFIX_BLOCKS + t
                )
            parts.append(self.kv[which, index, :, :])
        return jnp.concatenate(parts, 0)

    def rows(self, i):
        return aligned(i * STEP, STEP)

    def store_grad(self, t, i, value):
        for p in range(GROUP):
            self.grad[t, i * GROUP + p, :, :] = value[p * BLOCK:(p + 1) * BLOCK]

    def scores(self, t):
        length = self.lens[self.core * TURNS + t]
        shape = (TURN_LEN, ROWS)
        key_pos = lax.broadcasted_iota(jnp.int32, shape, 0)
        query_pos = lax.rem(lax.broadcasted_iota(jnp.int32, shape, 1), TURN_LEN)
        own_allowed = (key_pos <= query_pos) & (key_pos < length)

        def step(i, top):
            s = dot(self.blocks(t, 0, i), self.qs[t], 1, 1)
            own = jnp.where(own_allowed | (i < STEPS - 1), s[PREFIX_STEP:], -1e30)
            s = jnp.concatenate([s[:PREFIX_STEP], own], 0)
            self.score[self.rows(i), :] = s
            return jnp.maximum(top, fold(s, jnp.max))

        return step

    def exponentials(self, top):
        top = jnp.max(top, axis=0, keepdims=True) * EXP_SCALE

        def step(i, total):
            e = jnp.exp2(self.score[self.rows(i), :] * EXP_SCALE - top)
            self.score[self.rows(i), :] = e
            return total + fold(e, jnp.sum)

        total = lax.fori_loop(0, STEPS, step, jnp.zeros((8, ROWS), F32))
        return 1.0 / jnp.sum(total, axis=0, keepdims=True)

    def value_grads(self, t, scale, i):
        low = (self.score[self.rows(i), :] * scale).astype(BF16)
        self.prob[t, self.rows(i), :] = low
        self.store_grad(t, i, dot(low, self.gs[t], 1, 0))

    def probabilities(self):
        least = jnp.full((8, ROWS), -1e30, F32)
        scale = self.exponentials(lax.fori_loop(0, STEPS, self.scores(0), least))
        scores = self.scores(1)

        def step(i, top):
            self.value_grads(0, scale, i)
            return scores(i, top)

        scale_1 = self.exponentials(lax.fori_loop(0, STEPS, step, least))
        each(STEPS, lambda i: self.value_grads(1, scale_1, i))

    def score_grads(self, t, hook):
        gval, prob, qs, gs = self.score, self.prob, self.qs, self.gs

        def products(i, row_dot):
            v = dot(self.blocks(t, 1, i), gs[t], 1, 1)
            gval[self.rows(i), :] = v
            row_dot = row_dot + fold(prob[t, self.rows(i), :].astype(F32) * v, jnp.sum)
            hook(t * 2 * STEPS + i)
            return row_dot

        row_dot = lax.fori_loop(0, STEPS, products, jnp.zeros((8, ROWS), F32))
        row_dot = jnp.sum(row_dot, axis=0, keepdims=True)

        def key_grads(i):
            rows = self.rows(i)
            low = (prob[t, rows, :].astype(F32) * (gval[rows, :] - row_dot)).astype(BF16)
            prob[t, rows, :] = low
            self.store_grad(t, i, dot(low, qs[t], 1, 0) * INV_ROOT)
            hook((t * 2 + 1) * STEPS + i)

        each(STEPS, key_grads)

    def query_grads(self, t):
        self.dq[...] = jnp.zeros_like(self.dq)

        def step(i):
            self.dq[...] += dot(self.blocks(t, 0, i), self.prob[t, self.rows(i), :], 0, 0)

        each(STEPS, step)


def kernel(
    ids, lens, q_hbm, g_hbm, suf_hbm, kv_hbm, w_hbm,
    dq_hbm, dsuf_hbm, out_hbm,
    kv, q_own, q_peer, g_own, g_peer, qs, gs, suf, score, prob, grad, dq, dsuf,
    send, acc, r_first, r_second, r_third, x, named, inv,
    in_sems, s_in, s_out, out_sems, w_sems,
    s_core, s_legs, s_t, s_hops, s_own,
):
    hs = lax.axis_index("hs")
    grp = lax.axis_index("grp")
    core, head = lax.rem(hs, 2), hs // 2
    y, z = grp // 4, lax.rem(grp, 4)
    here = (y, lax.rem((z + 1) // 2, 2), z // 2)
    to_core = {"hs": head * 2 + 1 - core}
    along = (
        {"grp": (1 - y) * 4 + z},
        {"grp": y * 4 + z + 1 - 2 * lax.rem(z, 2)},
        {"grp": y * 4 + 3 - z},
    )

    def copy_to(source, target, send_sem, recv_sem, device):
        return pltpu.make_async_remote_copy(
            source, target, send_sem, recv_sem, device_id=device, device_id_type=MESH
        )

    def remote(source, target, sems, index, device):
        return copy_to(source, target, sems.at[(0, *index)], sems.at[(1, *index)], device)

    barrier = pltpu.get_barrier_semaphore()

    def greet(semaphore, device):
        pl.semaphore_signal(semaphore, inc=1, device_id=device, device_id_type=MESH)

    neighbours = (to_core, *along)
    for device in neighbours:
        greet(barrier, device)
    for j in range(1, KV_HEADS):
        greet(barrier, {"hs": lax.rem(head + j, KV_HEADS) * 2 + core})

    def turns_of(c):
        return aligned(c * MINE, MINE)

    columns = aligned(head * 2 * HEAD_DIM, 2 * HEAD_DIM)
    local = [
        pltpu.make_async_copy(kv_hbm, kv.at[core, pl.ds(0, PREFIX_BLOCKS)], in_sems.at[0]),
        pltpu.make_async_copy(q_hbm.at[turns_of(core), :], q_own, in_sems.at[1]),
        pltpu.make_async_copy(g_hbm.at[turns_of(core), :], g_own, in_sems.at[2]),
        pltpu.make_async_copy(suf_hbm.at[turns_of(core), columns], suf, in_sems.at[3]),
    ]
    for copy in local:
        copy.start()
    pl.semaphore_wait(barrier, 3 + KV_HEADS)
    far = [
        remote(q_hbm.at[turns_of(1 - core), :], q_peer, s_in, (0,), to_core),
        remote(g_hbm.at[turns_of(1 - core), :], g_peer, s_in, (1,), to_core),
    ]
    for j in range(COPIES):
        some = pl.ds(j * PREFIX_BLOCKS // COPIES, PREFIX_BLOCKS // COPIES)
        far.append(remote(kv_hbm.at[some], kv.at[core, some], s_in, (2 + j,), to_core))
    for copy in far:
        copy.start()
    for t in range(TURNS):
        grad[t, SLOTS, :, :] = jnp.zeros((BLOCK, HEAD_DIM), F32)

    turn_of = lax.broadcasted_iota(jnp.int32, named.shape, 0)
    block_of = lax.broadcasted_iota(jnp.int32, named.shape, 1)

    def name(p, table):
        for t in range(TURNS):
            hit = (turn_of == t) & (block_of == ids[core * TURNS + t, p])
            table = jnp.where(hit, p, table)
        return table

    named[...] = lax.fori_loop(0, PICKS, name, jnp.full(named.shape, SLOTS, jnp.int32))
    local.append(pltpu.make_async_copy(named, inv, in_sems.at[4]))
    local[-1].start()
    for copy in local[1:]:
        copy.wait()
    for copy in far[:2]:
        copy.wait()

    def lanes(j):
        return slice(j % OWN_HEADS * HEAD_DIM, (j % OWN_HEADS + 1) * HEAD_DIM)

    def stack(t):
        where = aligned(t * TURN_LEN, TURN_LEN)
        live = lax.broadcasted_iota(jnp.int32, (TURN_LEN, HEAD_DIM), 0) < lens[core * TURNS + t]
        for j in range(2 * OWN_HEADS):
            q_from, g_from = (q_own, g_own) if j < OWN_HEADS else (q_peer, g_peer)
            here = slice(j * TURN_LEN, (j + 1) * TURN_LEN)
            qs[t, here, :] = q_from[where, lanes(j)]
            g = g_from[where, lanes(j)]
            gs[t, here, :] = jnp.where(live, g, jnp.zeros_like(g))

    each(TURNS, stack)
    for t in range(TURNS):
        for which in range(2):
            own = suf[t * TURN_LEN:(t + 1) * TURN_LEN, which * HEAD_DIM:(which + 1) * HEAD_DIM]
            kv[which, PREFIX_BLOCKS + t, :, :] = own
    local[0].wait()
    for copy in far[2:]:
        copy.wait()

    def core_copy(f, c):
        return remote(send.at[c], acc.at[f, c], s_core, (f, c), to_core)

    def at(**fixed):
        return tuple(fixed.get(name, slice(None)) for name in ("d0", "d1", "d2"))

    def cube(directions, flip=()):
        return at(**{f"d{d}": 1 - here[d] if d in flip else here[d] for d in directions})

    landing = (r_first, r_second, r_third)

    def leg(f, c, order, step):
        index = cube(order[:step + 1], order[step:step + 1])
        return remote(
            acc.at[(f, c, *index)], landing[step].at[f, c], s_legs, (f, step, c), along[order[step]]
        )

    def leg_in(f, c, order, step):
        leg(f, c, order, step).wait_recv()
        index = (f, c, *cube(order[:step + 1]))
        total = acc[index].astype(F32) + landing[step][f, c].astype(F32)
        acc[index] = total.astype(BF16)

    def corner(b):
        return b // 4, b // 2 % 2, b % 2

    def dense(c, k, b):
        total = None
        for t in range(TURNS):
            slot = inv[t, (c * 2 + k) * RANGE_BLOCKS + b]
            term = grad[t, slot, :, :]
            total = term if total is None else total + term
        return total

    def send_core(f, c):
        for b in range(RANGE_BLOCKS):
            send[(c, *corner(b))] = dense(c, 1 - core, b).astype(BF16)
        core_copy(f, c).start()

    def sum_core(f, c):
        core_copy(f, c).wait_recv()
        for b in range(RANGE_BLOCKS):
            where = (f, c, *corner(b))
            acc[where] = (dense(c, core, b) + acc[where].astype(F32)).astype(BF16)

    def turn_out(f, c):
        return copy_to(
            acc.at[(f, c, *here)], x.at[(f, head, *here)],
            s_t.at[0, f, c], s_t.at[1, f, head], {"hs": c * 2 + core},
        )

    def turn_in(f, c):
        return copy_to(
            acc.at[(f, c, *here)], x.at[(f, c, *here)],
            s_t.at[0, f, c], s_t.at[1, f, c], {"hs": c * 2 + core},
        )

    def turn_own(f, c):
        return pltpu.make_async_copy(acc.at[(f, c, *here)], x.at[(f, c, *here)], s_own.at[f])

    def hand_on(f, c):
        @pl.when(c != head)
        def _():
            turn_out(f, c).start()

        @pl.when(c == head)
        def _():
            turn_own(f, c).start()

    def reduce_order(f, which):
        return turned_on(ORDERS[which], REDUCE_TURN[f])

    def first(which, i, f):
        c = SETS[which][0] + i
        sum_core(f, c)
        leg(f, c, reduce_order(f, which), 0).start()

    def later(which, i, f, step):
        c = SETS[which][0] + i
        leg_in(f, c, reduce_order(f, which), step - 1)
        leg(f, c, reduce_order(f, which), step).start()

    def last(which, i, f):
        c = SETS[which][0] + i
        leg_in(f, c, reduce_order(f, which), 2)
        hand_on(f, c)

    def row(i, step, *args):
        for which in range(len(SETS)):
            if i < SETS[which][1]:
                step(which, i, *args)

    def sent_core(f):
        each(KV_HEADS, lambda c: core_copy(f, c).wait_send())

    def sent_sets(f):
        def turned(c):
            @pl.when(c != head)
            def _():
                turn_out(f, c).wait_send()

        for which, (base, count) in enumerate(SETS):
            for step in range(3):
                each(count, lambda i: leg(f, base + i, reduce_order(f, which), step).wait_send())
        each(KV_HEADS, turned)

    def arrived(f, c):
        @pl.when(c != head)
        def _():
            turn_in(f, c).wait_recv()

        @pl.when(c == head)
        def _():
            turn_own(f, c).wait()

    PATHS = (((), 0), ((), 1), ((), 2), ((0,), 1), ((0,), 2), ((1,), 2), ((0, 1), 2))

    def hop(f, which, path):
        base, count = SETS[which]
        order = turned_on(ORDERS[which][::-1], GATHER_TURN[f])
        crossed, following = PATHS[path]
        index = cube((0, 1, 2), tuple(order[d] for d in crossed))
        block = x.at[(f, pl.ds(base, count), *index)]
        return remote(block, block, s_hops, (f, which, path), along[order[following]])

    def gather_first(f):
        for which, (base, count) in enumerate(SETS):
            each(count, lambda i: arrived(f, base + i))
            hop(f, which, 0).start()
        for path in (1, 2):
            for which in range(len(SETS)):
                hop(f, which, path).start()

    def gather_second(f):
        for which in range(len(SETS)):
            hop(f, which, 0).wait_recv()
            hop(f, which, 3).start()
            hop(f, which, 4).start()

    def gather_third(f):
        for which in range(len(SETS)):
            hop(f, which, 1).wait_recv()
            hop(f, which, 5).start()

    def gather_fourth(f):
        for which in range(len(SETS)):
            hop(f, which, 3).wait_recv()
            hop(f, which, 6).start()

    def gather_wait(f, *paths):
        for path in paths:
            for which in range(len(SETS)):
                hop(f, which, path).wait_recv()

    def sent_gather(f):
        for which in range(len(SETS)):
            for path in range(len(PATHS)):
                hop(f, which, path).wait_send()

    def w_copy(f, c):
        source = aligned(c * 2 * HEAD_DIM + (1 - f) * HEAD_DIM, HEAD_DIM)
        return pltpu.make_async_copy(
            w_hbm.at[:, source],
            prob.at[0, aligned(f * RANGE, RANGE), aligned(c * HEAD_DIM, HEAD_DIM)],
            w_sems.at[f, c],
        )

    def out_copy(place):
        rows = aligned((place[0] * 4 + place[1] * 2 + place[2]) * CHUNK, CHUNK)
        sem = out_sems.at[place[0] * 4 + place[1] * 2 + place[2]]
        return pltpu.make_async_copy(prob.at[1, rows, :], out_hbm.at[rows, :], sem)

    def product(f, places):
        left = jnp.concatenate(
            [
                jnp.concatenate([x[(f, c, *place)] for c in range(KV_HEADS)], 1)
                for place in places
            ],
            0,
        )
        return dot(left, prob[0, f * RANGE:(f + 1) * RANGE, :], 1, 1)

    def value_product(i):
        places = [(i // 2, lax.rem(i, 2), b) for b in range(2)]
        score[aligned(i * 2 * CHUNK, 2 * CHUNK), :] = product(0, places)

    def key_product(*flips):
        places = [cube((0, 1, 2), flip) for flip in flips]
        result = product(1, places)
        for j, place in enumerate(places):
            rows = aligned((place[0] * 4 + place[1] * 2 + place[2]) * CHUNK, CHUNK)
            total = score[rows, :] + result[j * CHUNK:(j + 1) * CHUNK]
            prob[1, rows, :] = total.astype(BF16)
            out_copy(place).start()

    work = Attention(core, ids, lens, kv, qs, gs, score, prob, grad, dq)
    work.probabilities()
    each(KV_HEADS, lambda c: send_core(0, c))

    def keep_value(t):
        dsuf[1, aligned(t * TURN_LEN, TURN_LEN), :] = grad[t, PICKS, :, :].astype(BF16)

    each(TURNS, keep_value)

    def firsts(f):
        def pair(i):
            for which in range(len(SETS)):
                first(which, i, f)

        each(2, pair)
        row(2, first, f)

    plan = {
        3: [lambda: row(0, later, 0, 1)],
        6: [lambda: row(1, later, 0, 1)],
        8: [lambda: row(2, later, 0, 1)],
        9: [lambda: row(0, later, 0, 2)],
        11: [lambda: row(1, later, 0, 2)],
    }

    def hook(n):
        for at, steps in plan.items():
            @pl.when(n == at)
            def _(steps=steps):
                for step in steps:
                    step()

    firsts(0)
    each(TURNS, lambda t: work.score_grads(t, hook))

    sent_core(0)
    each(KV_HEADS, lambda c: send_core(1, c))

    def keep_key(t):
        dsuf[0, aligned(t * TURN_LEN, TURN_LEN), :] = grad[t, PICKS, :, :].astype(BF16)

    each(TURNS, keep_key)
    row(2, later, 0, 2)
    row(0, last, 0)
    firsts(1)
    row(1, last, 0)
    row(2, last, 0)

    def query_out(t):
        work.query_grads(t)
        where = aligned(t * TURN_LEN, TURN_LEN)
        for j in range(2 * OWN_HEADS):
            target = q_own if j < OWN_HEADS else g_own
            part_t = dq[:, j * TURN_LEN:(j + 1) * TURN_LEN] * INV_ROOT
            target[where, lanes(j)] = part_t.T.astype(BF16)

    query_out(0)
    each(2, lambda f: each(KV_HEADS, lambda c: w_copy(f, c).start()))
    row(0, later, 1, 1)
    gather_first(0)
    query_out(1)
    results = [
        pltpu.make_async_copy(q_own, dq_hbm.at[turns_of(core), :], in_sems.at[0]),
        pltpu.make_async_copy(dsuf.at[core], dsuf_hbm.at[turns_of(core), :], in_sems.at[1]),
        remote(g_own, dq_hbm.at[turns_of(core), :], s_out, (0,), to_core),
        remote(dsuf.at[1 - core], dsuf_hbm.at[turns_of(core), :], s_out, (1,), to_core),
    ]
    for copy in results:
        copy.start()
    row(1, later, 1, 1)
    row(2, later, 1, 1)
    gather_second(0)
    row(0, later, 1, 2)
    gather_third(0)
    row(1, later, 1, 2)
    gather_fourth(0)
    row(2, later, 1, 2)
    row(0, last, 1)
    each(2, lambda f: each(KV_HEADS, lambda c: w_copy(f, c).wait()))
    row(1, last, 1)
    row(2, last, 1)
    gather_wait(0, 2, 4, 5, 6)
    each(4, value_product)

    gather_first(1)
    sent_core(1)
    sent_sets(0)
    gather_second(1)
    gather_third(1)
    gather_wait(1, 2)
    key_product((), (0,))
    gather_fourth(1)
    key_product((1,), (2,))
    sent_sets(1)
    sent_gather(0)
    for copy in results:
        copy.wait()
    gather_wait(1, 4, 5)
    key_product((0, 1), (0, 2))
    gather_wait(1, 6)
    key_product((1, 2), (0, 1, 2))

    sent_gather(1)
    each(PARTS, lambda i: out_copy((i // 4, lax.rem(i // 2, 2), lax.rem(i, 2))).wait())


def copy_kernel(*refs):
    count = (len(refs) - 2) // 3
    sources, targets, rooms = (refs[i * count:(i + 1) * count] for i in range(3))
    in_sems, out_sems = refs[-2:]

    def parts(make):
        index = 0
        for source, target, room in zip(sources, targets, rooms):
            rows = source.shape[0] // COPIES
            for j in range(COPIES):
                make(index, source, target, room, pl.ds(j * rows, rows))
                index += 1

    def read(index, source, target, room, where):
        return pltpu.make_async_copy(source.at[where, :], room.at[where, :], in_sems.at[index])

    def write(index, source, target, room, where):
        return pltpu.make_async_copy(room.at[where, :], target.at[where, :], out_sems.at[index])

    def pass_on(*args):
        read(*args).wait()
        write(*args).start()

    parts(lambda *args: read(*args).start())
    parts(pass_on)
    parts(lambda *args: write(*args).wait())


def separate(arrays):
    hbm = pl.BlockSpec(memory_space=pltpu.HBM)
    pieces = COPIES * len(arrays)
    return pl.pallas_call(
        copy_kernel,
        out_shape=[jax.ShapeDtypeStruct(array.shape, array.dtype) for array in arrays],
        in_specs=[hbm] * len(arrays),
        out_specs=[hbm] * len(arrays),
        scratch_shapes=[
            *(pltpu.VMEM(array.shape, array.dtype) for array in arrays),
            pltpu.SemaphoreType.DMA((pieces,)),
            pltpu.SemaphoreType.DMA((pieces,)),
        ],
        compiler_params=pltpu.CompilerParams(vmem_limit_bytes=64 * MIB),
        name="separate",
    )(*arrays)


def fused(ids, lens, q, g, suf, kv, weight):
    width = OWN_HEADS * HEAD_DIM
    dma = pltpu.SemaphoreType.DMA
    scratch = [
        pltpu.VMEM((2, PREFIX_BLOCKS + TURNS, BLOCK, HEAD_DIM), BF16),
        pltpu.VMEM((MINE, width), BF16),
        pltpu.VMEM((MINE, width), BF16),
        pltpu.VMEM((MINE, width), BF16),
        pltpu.VMEM((MINE, width), BF16),
        pltpu.VMEM((TURNS, ROWS, HEAD_DIM), BF16),
        pltpu.VMEM((TURNS, ROWS, HEAD_DIM), BF16),
        pltpu.VMEM((MINE, 2 * HEAD_DIM), BF16),
        pltpu.VMEM((KEYS, ROWS), F32),
        pltpu.VMEM((TURNS, KEYS, ROWS), BF16),
        pltpu.VMEM((TURNS, SLOTS + 1, BLOCK, HEAD_DIM), F32),
        pltpu.VMEM((HEAD_DIM, ROWS), F32),
        pltpu.VMEM((2, MINE, HEAD_DIM), BF16),
        pltpu.VMEM((KV_HEADS, 2, 2, 2, CHUNK, HEAD_DIM), BF16),
        pltpu.VMEM((2, KV_HEADS, 2, 2, 2, CHUNK, HEAD_DIM), BF16),
        pltpu.VMEM((2, KV_HEADS, 2, 2, CHUNK, HEAD_DIM), BF16),
        pltpu.VMEM((2, KV_HEADS, 2, CHUNK, HEAD_DIM), BF16),
        pltpu.VMEM((2, KV_HEADS, CHUNK, HEAD_DIM), BF16),
        pltpu.VMEM((2, KV_HEADS, 2, 2, 2, CHUNK, HEAD_DIM), BF16),
        pltpu.VMEM((8, PREFIX_BLOCKS), jnp.int32),
        pltpu.SMEM((8, PREFIX_BLOCKS), jnp.int32),
        dma((5,)),
        dma((2, 2 + COPIES)),
        dma((2, 2)),
        dma((PARTS,)),
        dma((2, KV_HEADS)),
        dma((2, 2, KV_HEADS)),
        dma((2, 2, 3, KV_HEADS)),
        dma((2, 2, KV_HEADS)),
        dma((2, 2, len(SETS), 7)),
        dma((2,)),
    ]
    return pl.pallas_call(
        kernel,
        out_shape=[
            jax.ShapeDtypeStruct((2 * MINE, width), BF16),
            jax.ShapeDtypeStruct((2 * MINE, HEAD_DIM), BF16),
            jax.ShapeDtypeStruct((RANGE, weight.shape[0]), BF16),
        ],
        in_specs=[SMEM, SMEM, HBM, HBM, HBM, HBM, HBM],
        out_specs=[HBM, HBM, HBM],
        scratch_shapes=scratch,
        compiler_params=pltpu.CompilerParams(
            collective_id=0, has_side_effects=True, vmem_limit_bytes=64 * MIB
        ),
        name="attention_backward",
    )(ids, lens, q, g, suf, kv.reshape(PREFIX_BLOCKS, BLOCK, HEAD_DIM), weight)


def on_device(queries, d_out, suffix_kv, prefix_kv, kv_weight, block_ids, lengths):
    return tuple(
        separate(
            fused(block_ids, lengths, queries, d_out, suffix_kv, prefix_kv, kv_weight)
        )
    )


def solution(mesh):
    placed = (
        P("grp", "hs"),
        P("grp", "hs"),
        P("grp", None),
        P(None, "hs"),
        P("grp", None),
        P("grp", None),
        P("grp"),
    )
    return jax.shard_map(
        on_device,
        mesh=mesh,
        in_specs=placed,
        out_specs=(P("grp", "hs"), P("grp", "hs"), P("hs", "grp")),
        check_vma=False,
    )
```
